512 devices in a mesh: tm: 256 (over z, x_lo, y, core), pts: 2 (over x_hi).
Axes of the slice: x: 4 (x_hi: 2, x_lo: 2; x = x_hi * 2 + x_lo), y: 8, z: 8, core: 2. Of those that a mesh axis runs over, the one named last changes fastest.
Arguments:
- features: bfloat16 [256, 64, 2048], P('tm', None, 'pts'), may hold values from -4.5 to 4.5
- positions: bfloat16 [256, 3, 2048], P('tm', None, 'pts'), may hold values from -6 to 6
- counts: int32 [256], replicated, may hold values from 512 to 2048, as said below
Outputs:
- velocity: float32 [256, 3, 2048], P('tm', None, 'pts')
The draws below stay inside these ranges and needn't reach their ends.
Inputs may be any that keep to these rules, and one draw needn't show every extreme that they name: The usable points of a frame are its first counts entries.
All inputs are finite; a program needn't handle non-finite values.
Results may differ from the reference program's by a relative error of at most 0.0003.
Values may be sent and summed in bfloat16 or wider, within the bound.
A program may use at most 64 MiB of HBM per device.

```python
import jax
import jax.numpy as jnp
from jax import lax

C = 64
P_SIZE = 2048
REACH = 3
FRAMES = 256


def draw_features(key, part):
    key = jax.random.fold_in(key, 11)
    key_base = jax.random.fold_in(key, 0)
    values = jnp.clip(jax.random.normal(key_base, (FRAMES, C, P_SIZE), jnp.float32), -4.5, 4.5)
    return values.astype(jnp.bfloat16)


def draw_counts(key, part):
    key = jax.random.fold_in(key, 5)
    key_values, key_order = jax.random.split(key)
    values = jax.random.randint(key_values, (FRAMES,), P_SIZE // 4, P_SIZE + 1)
    order = jax.random.permutation(key_order, FRAMES)
    values = values.at[order[0]].set(P_SIZE).at[order[1]].set(P_SIZE // 4)
    return values.astype(jnp.int32)


def level_of(own_key, dims, cuts, smallest, high):
    loudness = 1.0
    for dim, parts in cuts:
        steps = jax.random.uniform(jax.random.fold_in(jax.random.fold_in(own_key, 6), dim), (parts,), jnp.float32, smallest / len(cuts), high / len(cuts))
        loudness = loudness * jnp.repeat(jnp.exp(steps), dims[dim] // parts).reshape((-1,) + (1,) * (len(dims) - 1 - dim))
    return loudness


def bell_draw(stream_key, extent, spread, limit, cuts=(), kind=jnp.bfloat16):
    gain = level_of(stream_key, extent, cuts, -0.22, 0.18) if cuts else 1.0
    entries = jax.random.normal(stream_key, extent, jnp.float32) * spread * gain
    return jnp.minimum(jnp.maximum(entries, -limit), limit).astype(kind)


def setup_inputs(seed: int = 0) -> dict:
    seeds = jax.random.split(jax.random.key(seed), 4)
    return {
        "features": draw_features(jax.random.fold_in(seeds[3], 71), 0),
        "positions": bell_draw(seeds[1], (FRAMES, 3, P_SIZE), 1.0, 6.0, ((0, 256), (2, 2))),
        "counts": draw_counts(jax.random.fold_in(seeds[3], 71), 0),
    }


score_scale = 0.25
neg_big = -1.0e30


def pair_flows(src_feat, src_pos, src_usable, tgt_feat, tgt_pos, tgt_usable):
    scores = jnp.dot(src_feat.astype(jnp.float32).T, tgt_feat.astype(jnp.float32), precision=lax.Precision.HIGHEST) * score_scale
    src_coords = src_pos.astype(jnp.float32)
    tgt_coords = tgt_pos.astype(jnp.float32)
    row_masked = jnp.where(tgt_usable[None, :], scores, neg_big)
    row_peak = jnp.max(row_masked, axis=1, keepdims=True)
    row_weights = jnp.where(tgt_usable[None, :], jnp.exp(row_masked - row_peak), 0.0)
    row_summed = jnp.sum(row_weights, axis=1)
    row_acc = jnp.dot(tgt_coords, row_weights.T, precision=lax.Precision.HIGHEST)
    forward = jnp.where(src_usable[None, :], row_acc / row_summed[None, :] - src_coords, 0.0)
    col_masked = jnp.where(src_usable[:, None], scores, neg_big)
    col_peak = jnp.max(col_masked, axis=0, keepdims=True)
    col_weights = jnp.where(src_usable[:, None], jnp.exp(col_masked - col_peak), 0.0)
    col_summed = jnp.sum(col_weights, axis=0)
    col_acc = jnp.dot(src_coords, col_weights, precision=lax.Precision.HIGHEST)
    backward = jnp.where(tgt_usable[None, :], col_acc / col_summed[None, :] - tgt_coords, 0.0)
    return forward, backward


def reference(features, positions, counts):
    usable = jnp.arange(P_SIZE, dtype=jnp.int32)[None, :] < counts[:, None]
    velocity = jnp.zeros((FRAMES, 3, P_SIZE), jnp.float32)
    for offset in range(1, REACH + 1):
        def one_pair(frame_index):
            later_frame = frame_index + offset
            return pair_flows(features[frame_index], positions[frame_index], usable[frame_index],
                              features[later_frame], positions[later_frame], usable[later_frame])
        frame_ids = jnp.arange(FRAMES - offset, dtype=jnp.int32)
        forward, backward = lax.map(one_pair, frame_ids)
        velocity = velocity.at[:FRAMES - offset].add(forward / offset)
        velocity = velocity.at[offset:].add(-backward / offset)
    global_index = jnp.arange(FRAMES, dtype=jnp.int32)
    term_count = jnp.minimum(REACH, FRAMES - 1 - global_index) + jnp.minimum(REACH, global_index)
    return velocity / term_count.astype(jnp.float32)[:, None, None]
```

```python
import functools

import jax
import jax.numpy as jnp
from jax import lax
from jax.experimental import pallas as pl
from jax.experimental.pallas import tpu as pltpu
from jax.sharding import PartitionSpec as P

REACH = 3
CHANNELS = 64
HALF = 1024
PACK = HALF // 2
POS_ROWS = 32
MSG = PACK + POS_ROWS
SCORE_SCALE = 0.25
LOG2E = 1.4426950408889634
DEN_LOW = 2.0**-90
DEN_HIGH = 2.0**100
MESH = pl.DeviceIdType.MESH
f32 = jnp.float32
bf16 = jnp.bfloat16

OFFSETS = (1, 2, -1, -2, 3, -3)
FRAME_SLOTS = len(OFFSETS)
SLOTS = 2 * FRAME_SLOTS
XM = SLOTS


def wrapped(frame, total):
    return lax.rem(frame + total, total)


def pack_message(feat, pos, usable):
    kept = jnp.where(usable, feat.astype(f32), 0.0)
    rows = jnp.concatenate([kept[:, :PACK], kept[:, PACK:]], axis=0).T
    flag = usable.astype(f32)
    quad = jnp.concatenate([jnp.where(usable, pos.astype(f32), 0.0), flag], axis=0)
    tail = jnp.concatenate([quad[:, q * 128 : (q + 1) * 128] for q in range(HALF // 128)], axis=0)
    return rows.astype(bf16), tail.astype(bf16)


def position_rows(tail):
    tail = tail.astype(f32)
    pieces = []
    for j in range(POS_ROWS // 8):
        block = tail[j * 8 : j * 8 + 8]
        pieces.append(block)
        pieces.append(jnp.concatenate([block[4:], block[:4]], axis=0))
    return jnp.concatenate(pieces, axis=1).astype(bf16)


def gather_and_match(
    total, cnt_ref, feat_ref, pos_ref, out_ref, kept_ref, own, xm, keys, weights, acc, send_sem, recv_sem, keep_sem
):
    t = lax.axis_index("tm")
    p = lax.axis_index("pts")
    sigma = 1 - 2 * lax.rem(t, 2)
    sibling = wrapped(t + sigma, total)
    across = wrapped(t - sigma, total)
    near = wrapped(t - 2 * sigma, total)
    far = wrapped(t + 2 * sigma, total)
    partners = [(t, 1 - p), (sibling, p), (across, p), (near, p), (far, p)]

    barrier = pltpu.get_barrier_semaphore()
    for partner in partners:
        pl.semaphore_signal(barrier, inc=1, device_id=partner, device_id_type=MESH)

    point = lax.broadcasted_iota(jnp.int32, (1, HALF), 1) + p * HALF
    usable = point < cnt_ref[t]
    rows, tail = pack_message(feat_ref[0], pos_ref[0], usable)
    own[:PACK] = rows
    own[PACK:] = tail

    pl.semaphore_wait(barrier, len(partners))

    def send(src, slot, target):
        copy = pltpu.make_async_remote_copy(
            src_ref=src,
            dst_ref=xm if slot == XM else keys.at[slot],
            send_sem=send_sem.at[slot],
            recv_sem=recv_sem.at[slot],
            device_id=target,
            device_id_type=MESH,
        )
        copy.start()

    def arrived(dst, slot):
        pltpu.make_async_copy(dst, dst, recv_sem.at[slot]).wait()

    send(own, 0, (sibling, p))
    send(own, 1, (near, p))
    send(own, XM, (t, 1 - p))
    send(own, 3, (far, p))

    scaled = feat_ref[0].astype(f32) * (SCORE_SCALE * LOG2E)
    high = scaled.astype(bf16)
    low = (scaled - high.astype(f32)).astype(bf16)
    blank = jnp.zeros((CHANNELS, HALF), bf16)
    weights[0] = jnp.concatenate([high, blank, low, blank], axis=0)
    weights[1] = jnp.concatenate([blank, high, blank, low], axis=0)

    def step(u, carry):
        arrived(keys.at[u], u)

        @pl.when(u == 1)
        def _():
            send(keys.at[1], 2, (sibling, p))
            send(keys.at[1], 5, (across, p))

        @pl.when(u == 2)
        def _():
            arrived(xm, XM)
            send(xm, 7, (near, p))
            send(xm, 9, (far, p))
            send(xm, 6, (sibling, p))

        @pl.when(u == 3)
        def _():
            send(keys.at[3], 4, (sibling, p))

        @pl.when(u == 7)
        def _():
            send(keys.at[7], 8, (sibling, p))
            send(keys.at[7], 11, (across, p))

        @pl.when(u == 9)
        def _():
            send(keys.at[9], 10, (sibling, p))

        pltpu.make_async_copy(keys.at[u], kept_ref.at[u], keep_sem.at[u]).start()
        packed = keys[u, :PACK]
        packed = jnp.concatenate([packed, packed], axis=1)
        values = position_rows(keys[u, PACK:])
        highs, lows = [], []
        for half in range(2):
            scores = jnp.dot(packed, weights[half], preferred_element_type=f32)
            mass = jnp.exp2(scores)
            top = mass.astype(bf16)
            highs.append(top)
            lows.append((mass - top.astype(f32)).astype(bf16))
        acc[u] = jnp.dot(
            jnp.concatenate([values, values], axis=1),
            jnp.concatenate(highs + lows, axis=0),
            preferred_element_type=f32,
        )
        return carry

    lax.fori_loop(0, SLOTS, step, 0)

    coords = pos_ref[0].astype(f32)
    velocity = jnp.zeros((3, HALF), f32)
    sound = jnp.ones((1, HALF), f32)
    terms = jnp.minimum(REACH, total - 1 - t) + jnp.minimum(REACH, t)
    for slot, e in enumerate(OFFSETS):
        summed = acc[slot] + acc[slot + FRAME_SLOTS]
        den = summed[3:4]
        frame = t + e * sigma
        live = (frame >= 0) & (frame < total)
        fine = jnp.where((den > DEN_LOW) & (den < DEN_HIGH), 1.0, 0.0)
        sound = jnp.where(live, jnp.minimum(sound, fine), sound)
        share = sigma.astype(f32) / e
        velocity = velocity + jnp.where(live, (summed[:3] / den - coords) * share, 0.0)
    out_ref[0:3] = jnp.where(usable, velocity / terms.astype(f32), 0.0)
    out_ref[3:4] = jnp.where(usable, sound, 1.0)
    out_ref[4:8] = jnp.zeros((4, HALF), f32)

    def drain(slot, carry):
        pltpu.make_async_copy(keys.at[slot], kept_ref.at[slot], keep_sem.at[slot]).wait()
        pltpu.make_async_copy(own, own, send_sem.at[slot]).wait()
        return carry

    lax.fori_loop(0, SLOTS, drain, 0)
    pltpu.make_async_copy(own, own, send_sem.at[XM]).wait()


def finish(total, place_ref, cnt_ref, fast_ref, feat_ref, pos_ref, kept_ref, out_ref, feat, pos, block, stats, sem):
    sound = jnp.min(fast_ref[3:4]) > 0.5

    @pl.when(sound)
    def _():
        out_ref[0] = fast_ref[0:3]

    @pl.when(jnp.logical_not(sound))
    def _():
        t = place_ref[0]
        p = place_ref[1]
        sigma = 1 - 2 * lax.rem(t, 2)
        for src, dst in ((feat_ref, feat), (pos_ref, pos)):
            copy = pltpu.make_async_copy(src, dst, sem)
            copy.start()
            copy.wait()
        coords = pos[0].astype(f32)
        blank = jnp.zeros((CHANNELS, HALF), bf16)
        usable = lax.broadcasted_iota(jnp.int32, (1, HALF), 1) + p * HALF < cnt_ref[t]
        out_ref[0] = jnp.zeros((3, HALF), f32)
        terms = jnp.minimum(REACH, total - 1 - t) + jnp.minimum(REACH, t)

        def neighbour(slot, carry):
            size = jnp.where(slot < 2, slot + 1, jnp.where(slot < 4, slot - 1, 3))
            e = jnp.where((slot == 2) | (slot == 3) | (slot == 5), -size, size)
            frame = t + e * sigma
            live = (frame >= 0) & (frame < total)
            count = cnt_ref[wrapped(frame, total)]
            stats[0:8] = jnp.full((8, HALF), -1e30, f32)
            stats[8:16] = jnp.zeros((8, HALF), f32)

            def half_step(side, carry):
                copy = pltpu.make_async_copy(kept_ref.at[slot + side * FRAME_SLOTS], block, sem)
                copy.start()
                copy.wait()
                first = jnp.where(side == 0, p, 1 - p) * HALF
                values = position_rows(block[PACK:])
                for part in range(2):
                    query = [feat[0], blank] if part == 0 else [blank, feat[0]]
                    scores = (
                        jnp.dot(block[:PACK], jnp.concatenate(query, axis=0), preferred_element_type=f32)
                        * SCORE_SCALE
                    )
                    index = lax.broadcasted_iota(jnp.int32, (PACK, HALF), 0) + first + part * PACK
                    there = index < count
                    before = stats[0:1]
                    peak = jnp.maximum(before, jnp.max(jnp.where(there, scores, -1e30), axis=0, keepdims=True))
                    mass = jnp.where(there, jnp.exp(scores - peak), 0.0)
                    top = mass.astype(bf16)
                    rest = (mass - top.astype(f32)).astype(bf16)
                    lhs = values[:, part * PACK : (part + 1) * PACK]
                    fresh = jnp.dot(lhs, top, preferred_element_type=f32) + jnp.dot(
                        lhs, rest, preferred_element_type=f32
                    )
                    stats[8:16] = stats[8:16] * jnp.exp(before - peak) + fresh
                    stats[0:8] = jnp.broadcast_to(peak, (8, HALF))
                return carry

            lax.fori_loop(0, 2, half_step, 0)
            mean = stats[8:11] / stats[11:12]
            share = sigma.astype(f32) / e.astype(f32)
            out_ref[0] += jnp.where(live & usable, (mean - coords) * share, 0.0)
            return carry

        lax.fori_loop(0, FRAME_SLOTS, neighbour, 0)
        out_ref[0] = out_ref[0] / terms.astype(f32)


def per_device(features, positions, counts):
    total = counts.shape[0]
    vmem = pl.BlockSpec(memory_space=pltpu.VMEM)
    smem = pl.BlockSpec(memory_space=pltpu.SMEM)
    anywhere = pl.BlockSpec(memory_space=pl.ANY)
    fast, kept = pl.pallas_call(
        functools.partial(gather_and_match, total),
        out_shape=[
            jax.ShapeDtypeStruct((8, HALF), f32),
            jax.ShapeDtypeStruct((SLOTS, MSG, 128), bf16),
        ],
        in_specs=[smem, vmem, vmem],
        out_specs=[vmem, anywhere],
        scratch_shapes=[
            pltpu.VMEM((MSG, 128), bf16),
            pltpu.VMEM((MSG, 128), bf16),
            pltpu.VMEM((SLOTS, MSG, 128), bf16),
            pltpu.VMEM((2, 4 * CHANNELS, HALF), bf16),
            pltpu.VMEM((SLOTS, 8, HALF), f32),
            pltpu.SemaphoreType.DMA((SLOTS + 1,)),
            pltpu.SemaphoreType.DMA((SLOTS + 1,)),
            pltpu.SemaphoreType.DMA((SLOTS,)),
        ],
        compiler_params=pltpu.CompilerParams(
            collective_id=0, has_side_effects=True, vmem_limit_bytes=56 * 2**20
        ),
        name="gather_and_match",
    )(counts, features, positions)
    place = jnp.stack([lax.axis_index("tm"), lax.axis_index("pts")]).astype(jnp.int32)
    return pl.pallas_call(
        functools.partial(finish, total),
        out_shape=jax.ShapeDtypeStruct((1, 3, HALF), f32),
        in_specs=[smem, smem, vmem, anywhere, anywhere, anywhere],
        out_specs=vmem,
        scratch_shapes=[
            pltpu.VMEM((1, CHANNELS, HALF), bf16),
            pltpu.VMEM((1, 3, HALF), bf16),
            pltpu.VMEM((MSG, 128), bf16),
            pltpu.VMEM((16, HALF), f32),
            pltpu.SemaphoreType.DMA,
        ],
        compiler_params=pltpu.CompilerParams(vmem_limit_bytes=56 * 2**20),
        name="finish",
    )(place, counts, fast, features, positions, kept)


def solution(mesh):
    in_specs = (P("tm", None, "pts"), P("tm", None, "pts"), P())
    out_specs = P("tm", None, "pts")
    return jax.shard_map(
        per_device, mesh=mesh, in_specs=in_specs, out_specs=out_specs, check_vma=False
    )
```

```python
import functools

import jax
import jax.numpy as jnp
from jax import lax
from jax.experimental import pallas as pl
from jax.experimental.pallas import tpu as pltpu
from jax.sharding import PartitionSpec as P

REACH = 3
CHANNELS = 64
HALF = 1024
PACK = HALF // 2
POS_ROWS = 32
MSG = PACK + POS_ROWS
SCORE_SCALE = 0.25
LOG2E = 1.4426950408889634
DEN_LOW = 2.0**-90
DEN_HIGH = 2.0**100
MESH = pl.DeviceIdType.MESH
f32 = jnp.float32
bf16 = jnp.bfloat16

OFFSETS = (1, 2, -1, -2, 3, -3)
FRAME_SLOTS = len(OFFSETS)
SLOTS = 2 * FRAME_SLOTS
XM = SLOTS


def inside(frame, total):
    return (frame >= 0) & (frame < total)


def pack_message(feat, pos, usable):
    kept = jnp.where(usable, feat.astype(f32), 0.0)
    rows = jnp.concatenate([kept[:, :PACK], kept[:, PACK:]], axis=0).T
    flag = usable.astype(f32)
    quad = jnp.concatenate([jnp.where(usable, pos.astype(f32), 0.0), flag], axis=0)
    tail = jnp.concatenate([quad[:, q * 128 : (q + 1) * 128] for q in range(HALF // 128)], axis=0)
    return rows.astype(bf16), tail.astype(bf16)


def position_rows(tail):
    tail = tail.astype(f32)
    pieces = []
    for j in range(POS_ROWS // 8):
        block = tail[j * 8 : j * 8 + 8]
        pieces.append(block)
        pieces.append(jnp.concatenate([block[4:], block[:4]], axis=0))
    return jnp.concatenate(pieces, axis=1).astype(bf16)


def gather_and_match(
    total, cnt_ref, feat_ref, pos_ref, out_ref, kept_ref, own, xm, keys, weights, acc, send_sem, recv_sem, keep_sem
):
    t = lax.axis_index("tm")
    p = lax.axis_index("pts")
    sigma = 1 - 2 * lax.rem(t, 2)
    sibling, across, near, far = t + sigma, t - sigma, t - 2 * sigma, t + 2 * sigma

    barrier = pltpu.get_barrier_semaphore()
    pl.semaphore_signal(barrier, inc=1, device_id=(t, 1 - p), device_id_type=MESH)
    pl.semaphore_signal(barrier, inc=1, device_id=(sibling, p), device_id_type=MESH)
    partners = 2
    for frame in (across, near, far):
        partners = partners + inside(frame, total).astype(jnp.int32)

        @pl.when(inside(frame, total))
        def _():
            pl.semaphore_signal(barrier, inc=1, device_id=(frame, p), device_id_type=MESH)

    point = lax.broadcasted_iota(jnp.int32, (1, HALF), 1) + p * HALF
    usable = point < cnt_ref[t]
    rows, tail = pack_message(feat_ref[0], pos_ref[0], usable)
    own[:PACK] = rows
    own[PACK:] = tail

    pl.semaphore_wait(barrier, partners)

    def send(src, slot, frame, half):
        @pl.when(inside(frame, total))
        def _():
            pltpu.make_async_remote_copy(
                src_ref=src,
                dst_ref=xm if slot == XM else keys.at[slot],
                send_sem=send_sem.at[slot],
                recv_sem=recv_sem.at[slot],
                device_id=(frame, half),
                device_id_type=MESH,
            ).start()

    def arrived(dst, slot):
        pltpu.make_async_copy(dst, dst, recv_sem.at[slot]).wait()

    send(own, 0, sibling, p)
    send(own, 1, near, p)
    send(own, XM, t, 1 - p)
    send(own, 3, far, p)

    scaled = feat_ref[0].astype(f32) * (SCORE_SCALE * LOG2E)
    high = scaled.astype(bf16)
    low = (scaled - high.astype(f32)).astype(bf16)
    blank = jnp.zeros((CHANNELS, HALF), bf16)
    weights[0] = jnp.concatenate([high, blank, low, blank], axis=0)
    weights[1] = jnp.concatenate([blank, high, blank, low], axis=0)

    def frame_of(slot):
        place = lax.rem(slot, FRAME_SLOTS)
        size = jnp.where(place < 2, place + 1, jnp.where(place < 4, place - 1, 3))
        return t + sigma * jnp.where((place == 2) | (place == 3) | (place == 5), -size, size)

    def step(u, carry):
        @pl.when(u == 2)
        def _():
            arrived(xm, XM)
            send(xm, 7, near, p)
            send(xm, 9, far, p)
            send(xm, 6, sibling, p)

        @pl.when(inside(frame_of(u), total))
        def _():
            match(u)

        return carry

    def match(u):
        arrived(keys.at[u], u)

        @pl.when(u == 1)
        def _():
            send(keys.at[1], 2, sibling, p)
            send(keys.at[1], 5, across, p)

        @pl.when(u == 3)
        def _():
            send(keys.at[3], 4, sibling, p)

        @pl.when(u == 7)
        def _():
            send(keys.at[7], 8, sibling, p)
            send(keys.at[7], 11, across, p)

        @pl.when(u == 9)
        def _():
            send(keys.at[9], 10, sibling, p)

        pltpu.make_async_copy(keys.at[u], kept_ref.at[u], keep_sem.at[u]).start()
        packed = keys[u, :PACK]
        packed = jnp.concatenate([packed, packed], axis=1)
        values = position_rows(keys[u, PACK:])
        highs, lows = [], []
        for half in range(2):
            scores = jnp.dot(packed, weights[half], preferred_element_type=f32)
            mass = jnp.exp2(scores)
            top = mass.astype(bf16)
            highs.append(top)
            lows.append((mass - top.astype(f32)).astype(bf16))
        acc[u] = jnp.dot(
            jnp.concatenate([values, values], axis=1),
            jnp.concatenate(highs + lows, axis=0),
            preferred_element_type=f32,
        )

    lax.fori_loop(0, SLOTS, step, 0)

    coords = pos_ref[0].astype(f32)
    velocity = jnp.zeros((3, HALF), f32)
    sound = jnp.ones((1, HALF), f32)
    terms = jnp.minimum(REACH, total - 1 - t) + jnp.minimum(REACH, t)
    for slot, e in enumerate(OFFSETS):
        summed = acc[slot] + acc[slot + FRAME_SLOTS]
        den = summed[3:4]
        live = inside(t + e * sigma, total)
        fine = jnp.where((den > DEN_LOW) & (den < DEN_HIGH), 1.0, 0.0)
        sound = jnp.where(live, jnp.minimum(sound, fine), sound)
        share = sigma.astype(f32) / e
        velocity = velocity + jnp.where(live, (summed[:3] / den - coords) * share, 0.0)
    out_ref[0:3] = jnp.where(usable, velocity / terms.astype(f32), 0.0)
    out_ref[3:4] = jnp.where(usable, sound, 1.0)
    out_ref[4:8] = jnp.zeros((4, HALF), f32)

    def drain(slot, carry):
        @pl.when(inside(frame_of(slot), total))
        def _():
            pltpu.make_async_copy(keys.at[slot], kept_ref.at[slot], keep_sem.at[slot]).wait()

        return carry

    lax.fori_loop(0, SLOTS, drain, 0)

    def sent(slot, frame, condition=True):
        @pl.when(inside(frame, total) & condition)
        def _():
            pltpu.make_async_copy(own, own, send_sem.at[slot]).wait()

    ahead = inside(far, total)
    for side in (0, FRAME_SLOTS):
        sent(side + 0, sibling)
        sent(side + 1, near)
        sent(side + 3, far)
        sent(side + 2, sibling, ahead)
        sent(side + 5, across, ahead)
        sent(side + 4, sibling, inside(near, total))
    sent(XM, t)


def finish(total, cnt_ref, fast_ref, feat_ref, pos_ref, kept_ref, out_ref, feat, pos, block, stats, result, sem):
    sound = jnp.min(fast_ref[3:4]) > 0.5

    def put(values):
        for row in range(3):
            for q in range(HALF // 128):
                out_ref[row * 8 + q : row * 8 + q + 1] = values[row : row + 1, q * 128 : (q + 1) * 128]

    @pl.when(sound)
    def _():
        put(fast_ref[0:3])

    @pl.when(jnp.logical_not(sound))
    def _():
        t = lax.axis_index("tm")
        p = lax.axis_index("pts")
        sigma = 1 - 2 * lax.rem(t, 2)
        for src, dst in ((feat_ref, feat), (pos_ref, pos)):
            copy = pltpu.make_async_copy(src, dst, sem)
            copy.start()
            copy.wait()
        coords = pos[0].astype(f32)
        blank = jnp.zeros((CHANNELS, HALF), bf16)
        usable = lax.broadcasted_iota(jnp.int32, (1, HALF), 1) + p * HALF < cnt_ref[t]
        result[...] = jnp.zeros((8, HALF), f32)
        terms = jnp.minimum(REACH, total - 1 - t) + jnp.minimum(REACH, t)

        def neighbour(slot, carry):
            size = jnp.where(slot < 2, slot + 1, jnp.where(slot < 4, slot - 1, 3))
            e = jnp.where((slot == 2) | (slot == 3) | (slot == 5), -size, size)
            frame = t + e * sigma
            live = inside(frame, total)
            count = cnt_ref[jnp.clip(frame, 0, total - 1)]
            stats[0:8] = jnp.full((8, HALF), -1e30, f32)
            stats[8:16] = jnp.zeros((8, HALF), f32)

            def half_step(side, carry):
                copy = pltpu.make_async_copy(kept_ref.at[slot + side * FRAME_SLOTS], block, sem)
                copy.start()
                copy.wait()
                first = jnp.where(side == 0, p, 1 - p) * HALF
                values = position_rows(block[PACK:])
                for part in range(2):
                    query = [feat[0], blank] if part == 0 else [blank, feat[0]]
                    scores = (
                        jnp.dot(block[:PACK], jnp.concatenate(query, axis=0), preferred_element_type=f32)
                        * SCORE_SCALE
                    )
                    index = lax.broadcasted_iota(jnp.int32, (PACK, HALF), 0) + first + part * PACK
                    there = index < count
                    before = stats[0:1]
                    peak = jnp.maximum(before, jnp.max(jnp.where(there, scores, -1e30), axis=0, keepdims=True))
                    mass = jnp.where(there, jnp.exp(scores - peak), 0.0)
                    top = mass.astype(bf16)
                    rest = (mass - top.astype(f32)).astype(bf16)
                    lhs = values[:, part * PACK : (part + 1) * PACK]
                    fresh = jnp.dot(lhs, top, preferred_element_type=f32) + jnp.dot(
                        lhs, rest, preferred_element_type=f32
                    )
                    stats[8:16] = stats[8:16] * jnp.exp(before - peak) + fresh
                    stats[0:8] = jnp.broadcast_to(peak, (8, HALF))
                return carry

            lax.fori_loop(0, 2, half_step, 0)
            mean = stats[8:11] / stats[11:12]
            share = sigma.astype(f32) / e.astype(f32)
            result[0:3] += jnp.where(live & usable, (mean - coords) * share, 0.0)
            return carry

        lax.fori_loop(0, FRAME_SLOTS, neighbour, 0)
        put(result[0:3] / terms.astype(f32))


def per_device(features, positions, counts):
    total = counts.shape[0]
    vmem = pl.BlockSpec(memory_space=pltpu.VMEM)
    smem = pl.BlockSpec(memory_space=pltpu.SMEM)
    anywhere = pl.BlockSpec(memory_space=pl.ANY)
    fast, kept = pl.pallas_call(
        functools.partial(gather_and_match, total),
        out_shape=[
            jax.ShapeDtypeStruct((8, HALF), f32),
            jax.ShapeDtypeStruct((SLOTS, MSG, 128), bf16),
        ],
        in_specs=[smem, vmem, vmem],
        out_specs=[vmem, anywhere],
        scratch_shapes=[
            pltpu.VMEM((MSG, 128), bf16),
            pltpu.VMEM((MSG, 128), bf16),
            pltpu.VMEM((SLOTS, MSG, 128), bf16),
            pltpu.VMEM((2, 4 * CHANNELS, HALF), bf16),
            pltpu.VMEM((SLOTS, 8, HALF), f32),
            pltpu.SemaphoreType.DMA((SLOTS + 1,)),
            pltpu.SemaphoreType.DMA((SLOTS + 1,)),
            pltpu.SemaphoreType.DMA((SLOTS,)),
        ],
        compiler_params=pltpu.CompilerParams(
            collective_id=0, has_side_effects=True, vmem_limit_bytes=56 * 2**20
        ),
        name="gather_and_match",
    )(counts, features, positions)
    flat = pl.pallas_call(
        functools.partial(finish, total),
        out_shape=jax.ShapeDtypeStruct((3 * HALF // 128, 128), f32),
        in_specs=[smem, vmem, anywhere, anywhere, anywhere],
        out_specs=vmem,
        scratch_shapes=[
            pltpu.VMEM((1, CHANNELS, HALF), bf16),
            pltpu.VMEM((1, 3, HALF), bf16),
            pltpu.VMEM((MSG, 128), bf16),
            pltpu.VMEM((16, HALF), f32),
            pltpu.VMEM((8, HALF), f32),
            pltpu.SemaphoreType.DMA,
        ],
        compiler_params=pltpu.CompilerParams(vmem_limit_bytes=56 * 2**20),
        name="finish",
    )(counts, fast, features, positions, kept)
    return flat.reshape(1, 3, HALF)


def solution(mesh):
    in_specs = (P("tm", None, "pts"), P("tm", None, "pts"), P())
    out_specs = P("tm", None, "pts")
    return jax.shard_map(
        per_device, mesh=mesh, in_specs=in_specs, out_specs=out_specs, check_vma=False
    )
```

```python
import functools

import jax
import jax.numpy as jnp
from jax import lax
from jax.experimental import pallas as pl
from jax.experimental.pallas import tpu as pltpu
from jax.sharding import PartitionSpec as P

REACH = 3
CHANNELS = 64
HALF = 1024
PACK = HALF // 2
POS_ROWS = 32
MSG = PACK + POS_ROWS
SCORE_SCALE = 0.25
LOG2E = 1.4426950408889634
DEN_LOW = 2.0**6
DEN_HIGH = 2.0**24
ROW_FRAMES = 16
MESH = pl.DeviceIdType.MESH
f32 = jnp.float32
bf16 = jnp.bfloat16
f8 = jnp.float8_e5m2

OFFSETS = (1, 2, -2, -1, 3, -3)
FRAME_SLOTS = len(OFFSETS)
SLOTS = 2 * FRAME_SLOTS
XM = SLOTS
ORDERS = (
    (0, 1, 2, 3, 4, 5, 6, 7, 8, 9, 10, 11),
    (0, 1, 4, 6, 7, 10, 2, 3, 5, 8, 9, 11),
    (0, 2, 3, 5, 8, 6, 9, 11, 1, 4, 7, 10),
    (0, 1, 2, 3, 4, 6, 7, 8, 9, 10, 5, 11),
    (0, 1, 4, 6, 7, 10, 2, 3, 5, 8, 9, 11),
)
RELAY_STEPS = {
    1: (1, 1, 5, 1, 1),
    2: (2, 6, 1, 2, 6),
    XM: (2, 2, 2, 2, 4),
    7: (7, 4, 8, 6, 4),
    8: (7, 9, 4, 7, 9),
}
CROSS_STEP = 1


def inside(frame, total):
    return (frame >= 0) & (frame < total)


def pick(table, place):
    value = jnp.int32(table[-1])
    for index, entry in enumerate(table[:-1]):
        value = jnp.where(place == index, entry, value)
    return value


def other_row(a, b):
    return lax.div(a, ROW_FRAMES) != lax.div(b, ROW_FRAMES)


def pack_message(feat, pos, usable):
    kept = jnp.where(usable, feat.astype(f32), 0.0)
    rows = jnp.concatenate([kept[:, :PACK], kept[:, PACK:]], axis=0).astype(bf16).T
    flag = usable.astype(f32)
    quad = jnp.concatenate([jnp.where(usable, pos.astype(f32), 0.0), flag], axis=0)
    tail = jnp.concatenate([quad[:, q * 128 : (q + 1) * 128] for q in range(HALF // 128)], axis=0)
    return rows, tail.astype(bf16)


def position_rows(tail):
    tail = tail.astype(f32)
    pieces = []
    for j in range(POS_ROWS // 8):
        block = tail[j * 8 : j * 8 + 8]
        pieces.append(block)
        pieces.append(jnp.concatenate([block[4:], block[:4]], axis=0))
    return jnp.concatenate(pieces, axis=1).astype(bf16)


def gather_and_match(
    total,
    cnt_ref,
    feat_in,
    pos_in,
    out_ref,
    kept_ref,
    feat_ref,
    pos_ref,
    own,
    xm,
    keys,
    weights,
    acc,
    send_sem,
    recv_sem,
    keep_sem,
    load_sem,
):
    t = lax.axis_index("tm")
    p = lax.axis_index("pts")
    sigma = 1 - 2 * lax.rem(t, 2)
    sibling, across, near, far = t + sigma, t - sigma, t - 2 * sigma, t + 2 * sigma

    loads = [
        pltpu.make_async_copy(feat_in, feat_ref, load_sem.at[0]),
        pltpu.make_async_copy(pos_in, pos_ref, load_sem.at[1]),
    ]
    for load in loads:
        load.start()

    barrier = pltpu.get_barrier_semaphore()
    pl.semaphore_signal(barrier, inc=1, device_id=(t, 1 - p), device_id_type=MESH)
    pl.semaphore_signal(barrier, inc=1, device_id=(sibling, p), device_id_type=MESH)
    partners = 2
    for frame in (across, near, far):
        there = inside(frame, total)
        crossing = there & other_row(t, frame)
        partners = partners + there.astype(jnp.int32) + crossing.astype(jnp.int32)

        @pl.when(there)
        def _():
            pl.semaphore_signal(barrier, inc=1, device_id=(frame, p), device_id_type=MESH)

        @pl.when(crossing)
        def _():
            pl.semaphore_signal(barrier, inc=1, device_id=(frame, 1 - p), device_id_type=MESH)

    point = lax.broadcasted_iota(jnp.int32, (1, HALF), 1) + p * HALF
    usable = point < cnt_ref[t]
    for load in loads:
        load.wait()
    rows, tail = pack_message(feat_ref[0], pos_ref[0], usable)
    own[:PACK] = rows
    own[PACK:] = tail

    pl.semaphore_wait(barrier, partners)

    def send(src, slot, frame, half, condition=True):
        dst = xm if slot == XM else keys.at[slot]

        @pl.when(inside(frame, total) & condition)
        def _():
            pltpu.make_async_remote_copy(
                src_ref=src,
                dst_ref=dst,
                send_sem=send_sem.at[slot],
                recv_sem=recv_sem.at[slot],
                device_id=(frame, half),
                device_id_type=MESH,
            ).start()

    def arrived(dst, slot):
        pltpu.make_async_copy(dst, dst, recv_sem.at[slot]).wait()

    near_crosses, far_crosses, across_crosses = (other_row(t, frame) for frame in (near, far, across))
    send(own, 0, sibling, p)
    send(own, 1, near, p, jnp.logical_not(near_crosses))
    send(own, 2, far, p, jnp.logical_not(far_crosses))
    send(own, XM, t, 1 - p)

    scaled = feat_ref[0].astype(f32) * (SCORE_SCALE * LOG2E)
    high = scaled.astype(bf16)
    low = (scaled - high.astype(f32)).astype(bf16)
    weights[...] = jnp.concatenate([high, low], axis=0)

    def frame_of(slot):
        place = lax.rem(slot, FRAME_SLOTS)
        return t + sigma * pick(OFFSETS, place)

    place = lax.rem(t, ROW_FRAMES)
    mirrored = jnp.minimum(place, ROW_FRAMES - 1 - place)
    kind = jnp.where(mirrored < 3, mirrored + 1, 0)
    kind = jnp.where(lax.rem(t, 2 * ROW_FRAMES) == 0, 4, kind)

    def relay(step, slot):
        due = step == pick(RELAY_STEPS[slot], kind)
        if slot == XM:

            @pl.when(due)
            def _():
                arrived(xm, XM)
                send(xm, 6, sibling, p)
                send(xm, 7, near, p, jnp.logical_not(near_crosses))
                send(xm, 8, far, p, jnp.logical_not(far_crosses))
                send(own, 7, near, 1 - p, near_crosses)
                send(own, 8, far, 1 - p, far_crosses)

            return

        @pl.when(due & inside(frame_of(slot), total))
        def _():
            arrived(keys.at[slot], slot)
            if slot in (1, 7):
                send(keys.at[slot], slot + 2, sibling, p)
                send(keys.at[slot], slot + 4, across, p, True if slot == 1 else jnp.logical_not(across_crosses))
                if slot == 1:
                    send(keys.at[slot], 11, across, 1 - p, across_crosses)
            else:
                send(keys.at[slot], slot + 2, sibling, p)

    def step(index, carry):
        @pl.when(index == CROSS_STEP)
        def _():
            send(own, 1, near, p, near_crosses)
            send(own, 2, far, p, far_crosses)

        for slot in RELAY_STEPS:
            relay(index, slot)

        u = jnp.int32(0)
        for which, order in enumerate(ORDERS):
            u = jnp.where(kind == which, pick(order, index), u)

        @pl.when(inside(frame_of(u), total))
        def _():
            @pl.when((u != 1) & (u != 2) & (u != 7) & (u != 8))
            def _():
                arrived(keys.at[u], u)

            match(u)

        return carry

    def match(u):
        pltpu.make_async_copy(keys.at[u], kept_ref.at[u], keep_sem.at[u]).start()
        packed = keys[u, :PACK].astype(f32)
        turned = pltpu.roll(packed, CHANNELS, 1)
        left = lax.broadcasted_iota(jnp.int32, (PACK, 2 * CHANNELS), 1) < CHANNELS
        values = position_rows(keys[u, PACK:])
        highs, lows = [], []
        for half in range(2):
            points = jnp.where(left, packed, turned) if half == 0 else jnp.where(left, turned, packed)
            scores = jnp.dot(points.astype(bf16), weights[...], preferred_element_type=f32)
            mass = jnp.exp2(scores)
            top = mass.astype(bf16)
            highs.append(top)
            lows.append((mass - top.astype(f32)).astype(f8))
        acc[u] = jnp.dot(values, jnp.concatenate(highs, axis=0), preferred_element_type=f32) + jnp.dot(
            values.astype(f8), jnp.concatenate(lows, axis=0), preferred_element_type=f32
        )

    lax.fori_loop(0, SLOTS, step, 0)

    coords = pos_ref[0].astype(f32)
    velocity = jnp.zeros((3, HALF), f32)
    sound = jnp.ones((1, HALF), f32)
    terms = jnp.minimum(REACH, total - 1 - t) + jnp.minimum(REACH, t)
    for slot, e in enumerate(OFFSETS):
        summed = acc[slot] + acc[slot + FRAME_SLOTS]
        den = summed[3:4]
        live = inside(t + e * sigma, total)
        fine = jnp.where((den > DEN_LOW) & (den < DEN_HIGH), 1.0, 0.0)
        sound = jnp.where(live, jnp.minimum(sound, fine), sound)
        share = sigma.astype(f32) / e
        velocity = velocity + jnp.where(live, (summed[:3] / den - coords) * share, 0.0)
    out_ref[0:3] = jnp.where(usable, velocity / terms.astype(f32), 0.0)
    out_ref[3:4] = jnp.where(usable, sound, 1.0)
    out_ref[4:8] = jnp.zeros((4, HALF), f32)

    def drain(slot, carry):
        @pl.when(inside(frame_of(slot), total))
        def _():
            pltpu.make_async_copy(keys.at[slot], kept_ref.at[slot], keep_sem.at[slot]).wait()

        return carry

    lax.fori_loop(0, SLOTS, drain, 0)

    def sent(slot, frame, condition=True):
        @pl.when(inside(frame, total) & condition)
        def _():
            pltpu.make_async_copy(own, own, send_sem.at[slot]).wait()

    ahead = inside(far, total)
    for side in (0, FRAME_SLOTS):
        sent(side + 0, sibling)
        sent(side + 1, near)
        sent(side + 2, far)
        sent(side + 3, sibling, ahead)
        sent(side + 4, sibling, inside(near, total))
        sent(side + 5, across, ahead)
    sent(XM, t)


def finish(total, cnt_ref, fast_ref, feat_ref, pos_ref, kept_ref, out_ref, feat, pos, block, stats, result, sem):
    sound = jnp.min(fast_ref[3:4]) > 0.5

    def put(values):
        for row in range(3):
            for q in range(HALF // 128):
                out_ref[row * 8 + q : row * 8 + q + 1] = values[row : row + 1, q * 128 : (q + 1) * 128]

    @pl.when(sound)
    def _():
        put(fast_ref[0:3])

    @pl.when(jnp.logical_not(sound))
    def _():
        t = lax.axis_index("tm")
        p = lax.axis_index("pts")
        sigma = 1 - 2 * lax.rem(t, 2)
        for src, dst in ((feat_ref, feat), (pos_ref, pos)):
            copy = pltpu.make_async_copy(src, dst, sem)
            copy.start()
            copy.wait()
        coords = pos[0].astype(f32)
        blank = jnp.zeros((CHANNELS, HALF), bf16)
        usable = lax.broadcasted_iota(jnp.int32, (1, HALF), 1) + p * HALF < cnt_ref[t]
        result[...] = jnp.zeros((8, HALF), f32)
        terms = jnp.minimum(REACH, total - 1 - t) + jnp.minimum(REACH, t)

        def neighbour(slot, carry):
            e = pick(OFFSETS, slot)
            frame = t + e * sigma
            live = inside(frame, total)
            count = cnt_ref[jnp.clip(frame, 0, total - 1)]
            stats[0:8] = jnp.full((8, HALF), -1e30, f32)
            stats[8:16] = jnp.zeros((8, HALF), f32)

            def half_step(side, carry):
                copy = pltpu.make_async_copy(kept_ref.at[slot + side * FRAME_SLOTS], block, sem)
                copy.start()
                copy.wait()
                first = jnp.where(side == 0, p, 1 - p) * HALF
                values = position_rows(block[PACK:])
                for part in range(2):
                    query = [feat[0], blank] if part == 0 else [blank, feat[0]]
                    scores = (
                        jnp.dot(block[:PACK], jnp.concatenate(query, axis=0), preferred_element_type=f32)
                        * SCORE_SCALE
                    )
                    index = lax.broadcasted_iota(jnp.int32, (PACK, HALF), 0) + first + part * PACK
                    there = index < count
                    before = stats[0:1]
                    peak = jnp.maximum(before, jnp.max(jnp.where(there, scores, -1e30), axis=0, keepdims=True))
                    mass = jnp.where(there, jnp.exp(scores - peak), 0.0)
                    top = mass.astype(bf16)
                    rest = (mass - top.astype(f32)).astype(bf16)
                    lhs = values[:, part * PACK : (part + 1) * PACK]
                    fresh = jnp.dot(lhs, top, preferred_element_type=f32) + jnp.dot(
                        lhs, rest, preferred_element_type=f32
                    )
                    stats[8:16] = stats[8:16] * jnp.exp(before - peak) + fresh
                    stats[0:8] = jnp.broadcast_to(peak, (8, HALF))
                return carry

            lax.fori_loop(0, 2, half_step, 0)
            mean = stats[8:11] / stats[11:12]
            share = sigma.astype(f32) / e.astype(f32)
            result[0:3] += jnp.where(live & usable, (mean - coords) * share, 0.0)
            return carry

        lax.fori_loop(0, FRAME_SLOTS, neighbour, 0)
        put(result[0:3] / terms.astype(f32))


def per_device(features, positions, counts):
    total = counts.shape[0]
    vmem = pl.BlockSpec(memory_space=pltpu.VMEM)
    smem = pl.BlockSpec(memory_space=pltpu.SMEM)
    anywhere = pl.BlockSpec(memory_space=pl.ANY)
    fast, kept = pl.pallas_call(
        functools.partial(gather_and_match, total),
        out_shape=[
            jax.ShapeDtypeStruct((8, HALF), f32),
            jax.ShapeDtypeStruct((SLOTS, MSG, 128), bf16),
        ],
        in_specs=[smem, anywhere, anywhere],
        out_specs=[vmem, anywhere],
        scratch_shapes=[
            pltpu.VMEM((1, CHANNELS, HALF), bf16),
            pltpu.VMEM((1, 3, HALF), bf16),
            pltpu.VMEM((MSG, 128), bf16),
            pltpu.VMEM((MSG, 128), bf16),
            pltpu.VMEM((SLOTS, MSG, 128), bf16),
            pltpu.VMEM((2 * CHANNELS, HALF), bf16),
            pltpu.VMEM((SLOTS, 8, HALF), f32),
            pltpu.SemaphoreType.DMA((SLOTS + 1,)),
            pltpu.SemaphoreType.DMA((SLOTS + 1,)),
            pltpu.SemaphoreType.DMA((SLOTS,)),
            pltpu.SemaphoreType.DMA((2,)),
        ],
        compiler_params=pltpu.CompilerParams(
            collective_id=0, has_side_effects=True, vmem_limit_bytes=56 * 2**20
        ),
        name="gather_and_match",
    )(counts, features, positions)
    flat = pl.pallas_call(
        functools.partial(finish, total),
        out_shape=jax.ShapeDtypeStruct((3 * HALF // 128, 128), f32),
        in_specs=[smem, vmem, anywhere, anywhere, anywhere],
        out_specs=vmem,
        scratch_shapes=[
            pltpu.VMEM((1, CHANNELS, HALF), bf16),
            pltpu.VMEM((1, 3, HALF), bf16),
            pltpu.VMEM((MSG, 128), bf16),
            pltpu.VMEM((16, HALF), f32),
            pltpu.VMEM((8, HALF), f32),
            pltpu.SemaphoreType.DMA,
        ],
        compiler_params=pltpu.CompilerParams(vmem_limit_bytes=56 * 2**20),
        name="finish",
    )(counts, fast, features, positions, kept)
    return flat.reshape(1, 3, HALF)


def solution(mesh):
    in_specs = (P("tm", None, "pts"), P("tm", None, "pts"), P())
    out_specs = P("tm", None, "pts")
    return jax.shard_map(
        per_device, mesh=mesh, in_specs=in_specs, out_specs=out_specs, check_vma=False
    )
```

```python
import functools

import jax
import jax.numpy as jnp
from jax import lax
from jax.experimental import pallas as pl
from jax.experimental.pallas import tpu as pltpu
from jax.sharding import PartitionSpec as P

REACH = 3
CHANNELS = 64
HALF = 1024
PACK = HALF // 2
POS_ROWS = 32
MSG = PACK + POS_ROWS
SCORE_SCALE = 0.25
LOG2E = 1.4426950408889634
DEN_LOW = 2.0**6
DEN_HIGH = 2.0**24
ROW_FRAMES = 16
MESH = pl.DeviceIdType.MESH
f32 = jnp.float32
bf16 = jnp.bfloat16
f8 = jnp.float8_e5m2

OFFSETS = (1, 2, -2, -1, 3, -3)
FRAME_SLOTS = len(OFFSETS)
SLOTS = 2 * FRAME_SLOTS
XM = SLOTS
ORDERS = (
    (0, 1, 2, 3, 4, 5, 6, 7, 8, 9, 10, 11),
    (0, 1, 4, 6, 7, 10, 2, 3, 5, 8, 9, 11),
    (0, 2, 3, 6, 5, 8, 1, 9, 4, 7, 10, 11),
    (0, 1, 2, 3, 4, 6, 7, 8, 9, 10, 5, 11),
    (0, 2, 3, 6, 5, 8, 9, 1, 7, 4, 11, 10),
)
KINDS = (1, 2, 3, 0, 0, 0, 0, 0, 0, 0, 0, 0, 0, 3, 4, 1)
RELAY_STEPS = {
    1: (1, 1, 5, 1, 7),
    2: (2, 6, 1, 2, 1),
    XM: (3, 3, 3, 3, 3),
    7: (7, 4, 8, 6, 8),
    8: (7, 8, 5, 7, 5),
}
BACK_STEP = 3
CROSS_STEP = 1


def inside(frame, total):
    return (frame >= 0) & (frame < total)


def pick(table, place):
    value = jnp.int32(table[-1])
    for index, entry in enumerate(table[:-1]):
        value = jnp.where(place == index, entry, value)
    return value


def other_row(a, b):
    return lax.div(a, ROW_FRAMES) != lax.div(b, ROW_FRAMES)


def pack_message(feat, pos, usable):
    kept = jnp.where(usable, feat.astype(f32), 0.0)
    rows = jnp.concatenate([kept[:, :PACK], kept[:, PACK:]], axis=0).astype(bf16).T
    flag = usable.astype(f32)
    quad = jnp.concatenate([jnp.where(usable, pos.astype(f32), 0.0), flag], axis=0)
    tail = jnp.concatenate([quad[:, q * 128 : (q + 1) * 128] for q in range(HALF // 128)], axis=0)
    return rows, tail.astype(bf16)


def position_rows(tail):
    tail = tail.astype(f32)
    pieces = []
    for j in range(POS_ROWS // 8):
        block = tail[j * 8 : j * 8 + 8]
        pieces.append(block)
        pieces.append(jnp.concatenate([block[4:], block[:4]], axis=0))
    return jnp.concatenate(pieces, axis=1).astype(bf16)


def gather_and_match(
    total,
    cnt_in,
    feat_in,
    pos_in,
    out_ref,
    kept_ref,
    cnt_ref,
    feat_ref,
    pos_ref,
    own,
    xm,
    keys,
    weights,
    acc,
    send_sem,
    recv_sem,
    keep_sem,
    load_sem,
    half_ready,
    row_ready,
):
    t = lax.axis_index("tm")
    p = lax.axis_index("pts")
    sigma = 1 - 2 * lax.rem(t, 2)
    sibling, across, near, far = t + sigma, t - sigma, t - 2 * sigma, t + 2 * sigma

    loads = [
        pltpu.make_async_copy(feat_in, feat_ref, load_sem.at[0]),
        pltpu.make_async_copy(pos_in, pos_ref, load_sem.at[1]),
        pltpu.make_async_copy(cnt_in, cnt_ref, load_sem.at[2]),
    ]
    for load in loads:
        load.start()

    barrier = pltpu.get_barrier_semaphore()
    pl.semaphore_signal(barrier, inc=1, device_id=(sibling, p), device_id_type=MESH)
    awaited = 1 + p
    above, below = jnp.int32(0), jnp.int32(0)

    @pl.when(p == 0)
    def _():
        pl.semaphore_signal(barrier, inc=1, device_id=(t, 1 - p), device_id_type=MESH)

    for frame in (across, near, far):
        there = inside(frame, total)
        crossing = there & other_row(t, frame)
        same = there & jnp.logical_not(other_row(t, frame))
        awaited = awaited + same.astype(jnp.int32)
        above = above + (crossing & (frame > t)).astype(jnp.int32)
        below = below + (crossing & (frame < t)).astype(jnp.int32)

        @pl.when(same | (crossing & (frame < t)))
        def _():
            pl.semaphore_signal(barrier, inc=1, device_id=(frame, p), device_id_type=MESH)

        @pl.when(crossing & (frame < t))
        def _():
            pl.semaphore_signal(barrier, inc=1, device_id=(frame, 1 - p), device_id_type=MESH)

    point = lax.broadcasted_iota(jnp.int32, (1, HALF), 1) + p * HALF
    for load in loads:
        load.wait()
    usable = point < cnt_ref[t]
    rows, tail = pack_message(feat_ref[0], pos_ref[0], usable)
    own[:PACK] = rows
    own[PACK:] = tail

    pl.semaphore_wait(barrier, awaited + 2 * above)

    @pl.when(p == 1)
    def _():
        pl.semaphore_signal(half_ready, inc=1, device_id=(t, 1 - p), device_id_type=MESH)

    for frame in (across, near, far):

        @pl.when(inside(frame, total) & other_row(t, frame) & (frame > t))
        def _():
            for half in (p, 1 - p):
                pl.semaphore_signal(row_ready, inc=1, device_id=(frame, half), device_id_type=MESH)


    def send(src, slot, frame, half, condition=True):
        dst = xm if slot == XM else keys.at[slot]

        @pl.when(inside(frame, total) & condition)
        def _():
            pltpu.make_async_remote_copy(
                src_ref=src,
                dst_ref=dst,
                send_sem=send_sem.at[slot],
                recv_sem=recv_sem.at[slot],
                device_id=(frame, half),
                device_id_type=MESH,
            ).start()

    def arrived(dst, slot):
        pltpu.make_async_copy(dst, dst, recv_sem.at[slot]).wait()

    near_crosses, far_crosses, across_crosses = (other_row(t, frame) for frame in (near, far, across))
    send(own, 0, sibling, p)
    send(own, 1, near, p, jnp.logical_not(near_crosses))
    send(own, 2, far, p, jnp.logical_not(far_crosses))
    send(own, XM, t, 1 - p, p == 1)

    scaled = feat_ref[0].astype(f32) * (SCORE_SCALE * LOG2E)
    high = scaled.astype(bf16)
    low = (scaled - high.astype(f32)).astype(bf16)
    weights[...] = jnp.concatenate([high, low], axis=0)

    def frame_of(slot):
        place = lax.rem(slot, FRAME_SLOTS)
        return t + sigma * pick(OFFSETS, place)

    place = lax.rem(t, ROW_FRAMES)
    kind = pick(KINDS, place)

    def relay(step, slot):
        due = step == pick(RELAY_STEPS[slot], kind)
        if slot == XM:

            @pl.when(due)
            def _():
                arrived(xm, XM)
                send(xm, 6, sibling, p)
                send(xm, 7, near, p, jnp.logical_not(near_crosses))
                send(xm, 8, far, p, jnp.logical_not(far_crosses))
                send(own, 7, near, 1 - p, near_crosses & (near > t))
                send(own, 8, far, 1 - p, far_crosses & (far > t))

            return

        @pl.when(due & inside(frame_of(slot), total))
        def _():
            arrived(keys.at[slot], slot)
            if slot in (1, 7):
                send(keys.at[slot], slot + 2, sibling, p)
                if slot == 1:
                    ready = jnp.logical_not(across_crosses) | (across > t)
                    send(keys.at[slot], 5, across, p, ready)
                    send(keys.at[slot], 11, across, 1 - p, across_crosses & ready)
                else:
                    send(keys.at[slot], 11, across, p, jnp.logical_not(across_crosses))
            else:
                send(keys.at[slot], slot + 2, sibling, p)

    def step(index, carry):
        @pl.when(index == CROSS_STEP)
        def _():
            send(own, 1, near, p, near_crosses & (near > t))
            send(own, 2, far, p, far_crosses & (far > t))

        @pl.when((index == 0) & (p == 0))
        def _():
            pl.semaphore_wait(half_ready, 1)
            send(own, XM, t, 1 - p)

        for slot in RELAY_STEPS:
            relay(index, slot)

        @pl.when((index == BACK_STEP) & (below > 0))
        def _():
            pl.semaphore_wait(row_ready, 2 * below)
            send(own, 1, near, p, near_crosses)
            send(own, 2, far, p, far_crosses)
            send(own, 7, near, 1 - p, near_crosses)
            send(own, 8, far, 1 - p, far_crosses)
            for slot, half in ((5, p), (11, 1 - p)):
                send(keys.at[1], slot, across, half, across_crosses)

        u = jnp.int32(0)
        for which, order in enumerate(ORDERS):
            u = jnp.where(kind == which, pick(order, index), u)

        @pl.when(inside(frame_of(u), total))
        def _():
            @pl.when((u != 1) & (u != 2) & (u != 7) & (u != 8))
            def _():
                arrived(keys.at[u], u)

            match(u)

        return carry

    def match(u):
        pltpu.make_async_copy(keys.at[u], kept_ref.at[u], keep_sem.at[u]).start()
        packed = keys[u, :PACK].astype(f32)
        turned = pltpu.roll(packed, CHANNELS, 1)
        left = lax.broadcasted_iota(jnp.int32, (PACK, 2 * CHANNELS), 1) < CHANNELS
        values = position_rows(keys[u, PACK:])
        highs, lows = [], []
        for half in range(2):
            points = jnp.where(left, packed, turned) if half == 0 else jnp.where(left, turned, packed)
            scores = jnp.dot(points.astype(bf16), weights[...], preferred_element_type=f32)
            mass = jnp.exp2(scores)
            top = mass.astype(bf16)
            highs.append(top)
            lows.append((mass - top.astype(f32)).astype(f8))
        acc[u] = jnp.dot(values, jnp.concatenate(highs, axis=0), preferred_element_type=f32) + jnp.dot(
            values.astype(f8), jnp.concatenate(lows, axis=0), preferred_element_type=f32
        )

    lax.fori_loop(0, SLOTS, step, 0)

    coords = pos_ref[0].astype(f32)
    velocity = jnp.zeros((3, HALF), f32)
    sound = jnp.ones((1, HALF), f32)
    terms = jnp.minimum(REACH, total - 1 - t) + jnp.minimum(REACH, t)
    for slot, e in enumerate(OFFSETS):
        summed = acc[slot] + acc[slot + FRAME_SLOTS]
        den = summed[3:4]
        live = inside(t + e * sigma, total)
        fine = jnp.where((den > DEN_LOW) & (den < DEN_HIGH), 1.0, 0.0)
        sound = jnp.where(live, jnp.minimum(sound, fine), sound)
        share = sigma.astype(f32) / e
        velocity = velocity + jnp.where(live, (summed[:3] / den - coords) * share, 0.0)
    out_ref[0:3] = jnp.where(usable, velocity / terms.astype(f32), 0.0)
    out_ref[3:4] = jnp.where(usable, sound, 1.0)
    out_ref[4:8] = jnp.zeros((4, HALF), f32)

    def drain(slot, carry):
        @pl.when(inside(frame_of(slot), total))
        def _():
            pltpu.make_async_copy(keys.at[slot], kept_ref.at[slot], keep_sem.at[slot]).wait()

        return carry

    lax.fori_loop(0, SLOTS, drain, 0)

    def sent(slot, frame, condition=True):
        @pl.when(inside(frame, total) & condition)
        def _():
            pltpu.make_async_copy(own, own, send_sem.at[slot]).wait()

    ahead = inside(far, total)
    for side in (0, FRAME_SLOTS):
        sent(side + 0, sibling)
        sent(side + 1, near)
        sent(side + 2, far)
        sent(side + 3, sibling, ahead)
        sent(side + 4, sibling, inside(near, total))
        sent(side + 5, across, ahead)
    sent(XM, t)


def finish(total, cnt_ref, fast_ref, feat_ref, pos_ref, kept_ref, out_ref, feat, pos, block, stats, result, sem):
    sound = jnp.min(fast_ref[3:4]) > 0.5

    def put(values):
        for row in range(3):
            for q in range(HALF // 128):
                out_ref[row * 8 + q : row * 8 + q + 1] = values[row : row + 1, q * 128 : (q + 1) * 128]

    @pl.when(sound)
    def _():
        put(fast_ref[0:3])

    @pl.when(jnp.logical_not(sound))
    def _():
        t = lax.axis_index("tm")
        p = lax.axis_index("pts")
        sigma = 1 - 2 * lax.rem(t, 2)
        for src, dst in ((feat_ref, feat), (pos_ref, pos)):
            copy = pltpu.make_async_copy(src, dst, sem)
            copy.start()
            copy.wait()
        coords = pos[0].astype(f32)
        blank = jnp.zeros((CHANNELS, HALF), bf16)
        usable = lax.broadcasted_iota(jnp.int32, (1, HALF), 1) + p * HALF < cnt_ref[t]
        result[...] = jnp.zeros((8, HALF), f32)
        terms = jnp.minimum(REACH, total - 1 - t) + jnp.minimum(REACH, t)

        def neighbour(slot, carry):
            e = pick(OFFSETS, slot)
            frame = t + e * sigma
            live = inside(frame, total)
            count = cnt_ref[jnp.clip(frame, 0, total - 1)]
            stats[0:8] = jnp.full((8, HALF), -1e30, f32)
            stats[8:16] = jnp.zeros((8, HALF), f32)

            def half_step(side, carry):
                copy = pltpu.make_async_copy(kept_ref.at[slot + side * FRAME_SLOTS], block, sem)
                copy.start()
                copy.wait()
                first = jnp.where(side == 0, p, 1 - p) * HALF
                values = position_rows(block[PACK:])
                for part in range(2):
                    query = [feat[0], blank] if part == 0 else [blank, feat[0]]
                    scores = (
                        jnp.dot(block[:PACK], jnp.concatenate(query, axis=0), preferred_element_type=f32)
                        * SCORE_SCALE
                    )
                    index = lax.broadcasted_iota(jnp.int32, (PACK, HALF), 0) + first + part * PACK
                    there = index < count
                    before = stats[0:1]
                    peak = jnp.maximum(before, jnp.max(jnp.where(there, scores, -1e30), axis=0, keepdims=True))
                    mass = jnp.where(there, jnp.exp(scores - peak), 0.0)
                    top = mass.astype(bf16)
                    rest = (mass - top.astype(f32)).astype(bf16)
                    lhs = values[:, part * PACK : (part + 1) * PACK]
                    fresh = jnp.dot(lhs, top, preferred_element_type=f32) + jnp.dot(
                        lhs, rest, preferred_element_type=f32
                    )
                    stats[8:16] = stats[8:16] * jnp.exp(before - peak) + fresh
                    stats[0:8] = jnp.broadcast_to(peak, (8, HALF))
                return carry

            lax.fori_loop(0, 2, half_step, 0)
            mean = stats[8:11] / stats[11:12]
            share = sigma.astype(f32) / e.astype(f32)
            result[0:3] += jnp.where(live & usable, (mean - coords) * share, 0.0)
            return carry

        lax.fori_loop(0, FRAME_SLOTS, neighbour, 0)
        put(result[0:3] / terms.astype(f32))


def per_device(features, positions, counts):
    total = counts.shape[0]
    vmem = pl.BlockSpec(memory_space=pltpu.VMEM)
    smem = pl.BlockSpec(memory_space=pltpu.SMEM)
    anywhere = pl.BlockSpec(memory_space=pl.ANY)
    fast, kept = pl.pallas_call(
        functools.partial(gather_and_match, total),
        out_shape=[
            jax.ShapeDtypeStruct((8, HALF), f32),
            jax.ShapeDtypeStruct((SLOTS, MSG, 128), bf16),
        ],
        in_specs=[anywhere, anywhere, anywhere],
        out_specs=[vmem, anywhere],
        scratch_shapes=[
            pltpu.SMEM((total,), jnp.int32),
            pltpu.VMEM((1, CHANNELS, HALF), bf16),
            pltpu.VMEM((1, 3, HALF), bf16),
            pltpu.VMEM((MSG, 128), bf16),
            pltpu.VMEM((MSG, 128), bf16),
            pltpu.VMEM((SLOTS, MSG, 128), bf16),
            pltpu.VMEM((2 * CHANNELS, HALF), bf16),
            pltpu.VMEM((SLOTS, 8, HALF), f32),
            pltpu.SemaphoreType.DMA((SLOTS + 1,)),
            pltpu.SemaphoreType.DMA((SLOTS + 1,)),
            pltpu.SemaphoreType.DMA((SLOTS,)),
            pltpu.SemaphoreType.DMA((3,)),
            pltpu.SemaphoreType.REGULAR,
            pltpu.SemaphoreType.REGULAR,
        ],
        compiler_params=pltpu.CompilerParams(
            collective_id=0, has_side_effects=True, vmem_limit_bytes=56 * 2**20
        ),
        name="gather_and_match",
    )(counts, features, positions)
    flat = pl.pallas_call(
        functools.partial(finish, total),
        out_shape=jax.ShapeDtypeStruct((3 * HALF // 128, 128), f32),
        in_specs=[smem, vmem, anywhere, anywhere, anywhere],
        out_specs=vmem,
        scratch_shapes=[
            pltpu.VMEM((1, CHANNELS, HALF), bf16),
            pltpu.VMEM((1, 3, HALF), bf16),
            pltpu.VMEM((MSG, 128), bf16),
            pltpu.VMEM((16, HALF), f32),
            pltpu.VMEM((8, HALF), f32),
            pltpu.SemaphoreType.DMA,
        ],
        compiler_params=pltpu.CompilerParams(vmem_limit_bytes=56 * 2**20),
        name="finish",
    )(counts, fast, features, positions, kept)
    return flat.reshape(1, 3, HALF)


def solution(mesh):
    in_specs = (P("tm", None, "pts"), P("tm", None, "pts"), P())
    out_specs = P("tm", None, "pts")
    return jax.shard_map(
        per_device, mesh=mesh, in_specs=in_specs, out_specs=out_specs, check_vma=False
    )
```

```python
import functools

import jax
import jax.numpy as jnp
from jax import lax
from jax.experimental import pallas as pl
from jax.experimental.pallas import tpu as pltpu
from jax.sharding import PartitionSpec as P

REACH = 3
CHANNELS = 64
HALF = 1024
PACK = HALF // 2
POS_ROWS = 32
MSG = PACK + POS_ROWS
ROWS = 3 * HALF // 128
FLAG_ROWS = HALF // 128
SCORE_SCALE = 0.25
LOG2E = 1.4426950408889634
DEN_LOW = 2.0**6
DEN_HIGH = 2.0**24
ROW_FRAMES = 16
MESH = pl.DeviceIdType.MESH
f32 = jnp.float32
bf16 = jnp.bfloat16
f8 = jnp.float8_e5m2

OFFSETS = (1, 2, -2, -1, 3, -3)
FRAME_SLOTS = len(OFFSETS)
SLOTS = 2 * FRAME_SLOTS
XM = SLOTS
ORDERS = (
    (0, 1, 2, 3, 4, 5, 6, 7, 8, 9, 10, 11),
    (0, 1, 4, 6, 7, 10, 2, 3, 8, 5, 9, 11),
    (0, 2, 3, 6, 5, 8, 1, 9, 4, 7, 10, 11),
    (0, 1, 2, 3, 4, 6, 7, 8, 9, 10, 5, 11),
    (0, 2, 3, 6, 5, 8, 9, 1, 7, 4, 11, 10),
    (0, 1, 4, 6, 7, 2, 10, 3, 8, 5, 9, 11),
    (0, 2, 3, 5, 8, 6, 9, 11, 1, 4, 7, 10),
)
KINDS = (1, 2, 3, 0, 0, 0, 0, 0, 0, 0, 0, 0, 0, 3, 4, 5)
RELAY_STEPS = {
    1: (1, 1, 5, 1, 7, 1, 8),
    2: (2, 6, 1, 2, 1, 5, 1),
    XM: (3, 3, 3, 3, 3, 3, 3),
    7: (7, 4, 8, 6, 8, 4, 10),
    8: (7, 8, 5, 7, 5, 8, 4),
}
BACK_STEP = 3
CROSS_STEP = 1


def inside(frame, total):
    return (frame >= 0) & (frame < total)


def pick(table, place):
    value = jnp.int32(table[-1])
    for index, entry in enumerate(table[:-1]):
        value = jnp.where(place == index, entry, value)
    return value


def other_row(a, b):
    return lax.div(a, ROW_FRAMES) != lax.div(b, ROW_FRAMES)


def pack_message(feat, pos, usable):
    kept = jnp.where(usable, feat.astype(f32), 0.0)
    rows = jnp.concatenate([kept[:, :PACK], kept[:, PACK:]], axis=0).astype(bf16).T
    flag = usable.astype(f32)
    quad = jnp.concatenate([jnp.where(usable, pos.astype(f32), 0.0), flag], axis=0)
    tail = jnp.concatenate([quad[:, q * 128 : (q + 1) * 128] for q in range(HALF // 128)], axis=0)
    return rows, tail.astype(bf16)


def position_rows(tail):
    tail = tail.astype(f32)
    pieces = []
    for j in range(POS_ROWS // 8):
        block = tail[j * 8 : j * 8 + 8]
        pieces.append(block)
        pieces.append(jnp.concatenate([block[4:], block[:4]], axis=0))
    return jnp.concatenate(pieces, axis=1).astype(bf16)


def put_rows(ref, values, first):
    for row in range(values.shape[0]):
        for q in range(HALF // 128):
            at = first + row * (HALF // 128) + q
            ref[at : at + 1] = values[row : row + 1, q * 128 : (q + 1) * 128]


def gather_and_match(
    total,
    cnt_in,
    feat_in,
    pos_in,
    out_ref,
    kept_ref,
    cnt_ref,
    feat_ref,
    pos_ref,
    own,
    xm,
    keys,
    weights,
    acc,
    send_sem,
    recv_sem,
    keep_sem,
    load_sem,
    half_ready,
    row_ready,
    result,
    result_sem,
):
    t = lax.axis_index("tm")
    p = lax.axis_index("pts")
    sigma = 1 - 2 * lax.rem(t, 2)
    sibling, across, near, far = t + sigma, t - sigma, t - 2 * sigma, t + 2 * sigma

    loads = [
        pltpu.make_async_copy(feat_in, feat_ref, load_sem.at[0]),
        pltpu.make_async_copy(pos_in, pos_ref, load_sem.at[1]),
        pltpu.make_async_copy(cnt_in, cnt_ref, load_sem.at[2]),
    ]
    for load in loads:
        load.start()

    barrier = pltpu.get_barrier_semaphore()
    pl.semaphore_signal(barrier, inc=1, device_id=(sibling, p), device_id_type=MESH)
    awaited = 1 + p
    above, below = jnp.int32(0), jnp.int32(0)

    @pl.when(p == 0)
    def _():
        pl.semaphore_signal(barrier, inc=1, device_id=(t, 1 - p), device_id_type=MESH)

    for frame in (across, near, far):
        there = inside(frame, total)
        crossing = there & other_row(t, frame)
        same = there & jnp.logical_not(other_row(t, frame))
        awaited = awaited + same.astype(jnp.int32)
        above = above + (crossing & (frame > t)).astype(jnp.int32)
        below = below + (crossing & (frame < t)).astype(jnp.int32)

        @pl.when(same | (crossing & (frame < t)))
        def _():
            pl.semaphore_signal(barrier, inc=1, device_id=(frame, p), device_id_type=MESH)

        @pl.when(crossing & (frame < t))
        def _():
            pl.semaphore_signal(barrier, inc=1, device_id=(frame, 1 - p), device_id_type=MESH)

    point = lax.broadcasted_iota(jnp.int32, (1, HALF), 1) + p * HALF
    for load in loads:
        load.wait()
    usable = point < cnt_ref[t]
    rows, tail = pack_message(feat_ref[0], pos_ref[0], usable)
    own[:PACK] = rows
    own[PACK:] = tail

    pl.semaphore_wait(barrier, awaited + 2 * above)

    @pl.when(p == 1)
    def _():
        pl.semaphore_signal(half_ready, inc=1, device_id=(t, 1 - p), device_id_type=MESH)

    for frame in (across, near, far):

        @pl.when(inside(frame, total) & other_row(t, frame) & (frame > t))
        def _():
            for half in (p, 1 - p):
                pl.semaphore_signal(row_ready, inc=1, device_id=(frame, half), device_id_type=MESH)


    def send(src, slot, frame, half, condition=True):
        dst = xm if slot == XM else keys.at[slot]

        @pl.when(inside(frame, total) & condition)
        def _():
            pltpu.make_async_remote_copy(
                src_ref=src,
                dst_ref=dst,
                send_sem=send_sem.at[slot],
                recv_sem=recv_sem.at[slot],
                device_id=(frame, half),
                device_id_type=MESH,
            ).start()

    def arrived(dst, slot):
        pltpu.make_async_copy(dst, dst, recv_sem.at[slot]).wait()

    near_crosses, far_crosses, across_crosses = (other_row(t, frame) for frame in (near, far, across))
    send(own, 0, sibling, p)
    send(own, 1, near, p, jnp.logical_not(near_crosses))
    send(own, 2, far, p, jnp.logical_not(far_crosses))
    send(own, XM, t, 1 - p, p == 1)

    scaled = feat_ref[0].astype(f32) * (SCORE_SCALE * LOG2E)
    high = scaled.astype(bf16)
    low = (scaled - high.astype(f32)).astype(bf16)
    weights[...] = jnp.concatenate([high, low], axis=0)

    def frame_of(slot):
        place = lax.rem(slot, FRAME_SLOTS)
        return t + sigma * pick(OFFSETS, place)

    place = lax.rem(t, ROW_FRAMES)
    kind = jnp.where(t == 1, 6, pick(KINDS, place))

    def relay(step, slot):
        due = step == pick(RELAY_STEPS[slot], kind)
        if slot == XM:

            @pl.when(due)
            def _():
                arrived(xm, XM)
                send(xm, 6, sibling, p)
                send(xm, 7, near, p, jnp.logical_not(near_crosses))
                send(xm, 8, far, p, jnp.logical_not(far_crosses))
                send(own, 7, near, 1 - p, near_crosses & (near > t))
                send(own, 8, far, 1 - p, far_crosses & (far > t))

            return

        @pl.when(due & inside(frame_of(slot), total))
        def _():
            arrived(keys.at[slot], slot)
            if slot in (1, 7):
                send(keys.at[slot], slot + 2, sibling, p)
                if slot == 1:
                    ready = jnp.logical_not(across_crosses) | (across > t)
                    send(keys.at[slot], 5, across, p, ready)
                    send(keys.at[slot], 11, across, 1 - p, across_crosses & ready)
                else:
                    send(keys.at[slot], 11, across, p, jnp.logical_not(across_crosses))
            else:
                send(keys.at[slot], slot + 2, sibling, p)

    def step(index, carry):
        @pl.when(index == CROSS_STEP)
        def _():
            send(own, 1, near, p, near_crosses & (near > t))
            send(own, 2, far, p, far_crosses & (far > t))

        @pl.when((index == 0) & (p == 0))
        def _():
            pl.semaphore_wait(half_ready, 1)
            send(own, XM, t, 1 - p)

        for slot in RELAY_STEPS:
            relay(index, slot)

        @pl.when((index == BACK_STEP) & (below > 0))
        def _():
            pl.semaphore_wait(row_ready, 2 * below)
            send(own, 1, near, p, near_crosses)
            send(own, 2, far, p, far_crosses)
            send(own, 7, near, 1 - p, near_crosses)
            send(own, 8, far, 1 - p, far_crosses)
            for slot, half in ((5, p), (11, 1 - p)):
                send(keys.at[1], slot, across, half, across_crosses)

        u = jnp.int32(0)
        for which, order in enumerate(ORDERS):
            u = jnp.where(kind == which, pick(order, index), u)

        @pl.when(inside(frame_of(u), total))
        def _():
            @pl.when((u != 1) & (u != 2) & (u != 7) & (u != 8))
            def _():
                arrived(keys.at[u], u)

            match(u)

        return carry

    def match(u):
        pltpu.make_async_copy(keys.at[u], kept_ref.at[u], keep_sem.at[u]).start()
        packed = keys[u, :PACK].astype(f32)
        turned = pltpu.roll(packed, CHANNELS, 1)
        left = lax.broadcasted_iota(jnp.int32, (PACK, 2 * CHANNELS), 1) < CHANNELS
        values = position_rows(keys[u, PACK:])
        highs, lows = [], []
        for half in range(2):
            points = jnp.where(left, packed, turned) if half == 0 else jnp.where(left, turned, packed)
            scores = jnp.dot(points.astype(bf16), weights[...], preferred_element_type=f32)
            mass = jnp.exp2(scores)
            top = mass.astype(bf16)
            highs.append(top)
            lows.append((mass - top.astype(f32)).astype(f8))
        acc[u] = jnp.dot(values, jnp.concatenate(highs, axis=0), preferred_element_type=f32) + jnp.dot(
            values.astype(f8), jnp.concatenate(lows, axis=0), preferred_element_type=f32
        )

    lax.fori_loop(0, SLOTS, step, 0)

    coords = pos_ref[0].astype(f32)
    velocity = jnp.zeros((3, HALF), f32)
    sound = jnp.ones((1, HALF), f32)
    terms = jnp.minimum(REACH, total - 1 - t) + jnp.minimum(REACH, t)
    for slot, e in enumerate(OFFSETS):
        summed = acc[slot] + acc[slot + FRAME_SLOTS]
        den = summed[3:4]
        live = inside(t + e * sigma, total)
        fine = jnp.where((den > DEN_LOW) & (den < DEN_HIGH), 1.0, 0.0)
        sound = jnp.where(live, jnp.minimum(sound, fine), sound)
        share = sigma.astype(f32) / e
        velocity = velocity + jnp.where(live, (summed[:3] / den - coords) * share, 0.0)
    put_rows(result, jnp.where(usable, velocity / terms.astype(f32), 0.0), 0)
    put_rows(result, jnp.where(usable, sound, 1.0), ROWS)
    leave = pltpu.make_async_copy(result, out_ref, result_sem)
    leave.start()

    def drain(slot, carry):
        @pl.when(inside(frame_of(slot), total))
        def _():
            pltpu.make_async_copy(keys.at[slot], kept_ref.at[slot], keep_sem.at[slot]).wait()

        return carry

    lax.fori_loop(0, SLOTS, drain, 0)

    def sent(slot, frame, condition=True):
        @pl.when(inside(frame, total) & condition)
        def _():
            pltpu.make_async_copy(own, own, send_sem.at[slot]).wait()

    ahead = inside(far, total)
    for side in (0, FRAME_SLOTS):
        sent(side + 0, sibling)
        sent(side + 1, near)
        sent(side + 2, far)
        sent(side + 3, sibling, ahead)
        sent(side + 4, sibling, inside(near, total))
        sent(side + 5, across, ahead)
    sent(XM, t)
    leave.wait()


def finish(
    total, cnt_in, fast_ref, feat_ref, pos_ref, kept_ref, out_ref, cnt_ref, flags, feat, pos, block, stats, result, lines, sem
):
    whole = pltpu.make_async_copy(fast_ref.at[pl.ds(0, ROWS)], out_ref, sem.at[0])
    check = pltpu.make_async_copy(fast_ref.at[pl.ds(ROWS, FLAG_ROWS)], flags, sem.at[1])
    check.start()
    whole.start()
    check.wait()
    sound = jnp.min(flags[...]) > 0.5
    whole.wait()

    @pl.when(jnp.logical_not(sound))
    def _():
        t = lax.axis_index("tm")
        p = lax.axis_index("pts")
        sigma = 1 - 2 * lax.rem(t, 2)
        for src, dst in ((feat_ref, feat), (pos_ref, pos), (cnt_in, cnt_ref)):
            copy = pltpu.make_async_copy(src, dst, sem.at[0])
            copy.start()
            copy.wait()
        coords = pos[0].astype(f32)
        blank = jnp.zeros((CHANNELS, HALF), bf16)
        usable = lax.broadcasted_iota(jnp.int32, (1, HALF), 1) + p * HALF < cnt_ref[t]
        result[...] = jnp.zeros((8, HALF), f32)
        terms = jnp.minimum(REACH, total - 1 - t) + jnp.minimum(REACH, t)

        def neighbour(slot, carry):
            e = pick(OFFSETS, slot)
            frame = t + e * sigma
            live = inside(frame, total)
            count = cnt_ref[jnp.clip(frame, 0, total - 1)]
            stats[0:8] = jnp.full((8, HALF), -1e30, f32)
            stats[8:16] = jnp.zeros((8, HALF), f32)

            def half_step(side, carry):
                copy = pltpu.make_async_copy(kept_ref.at[slot + side * FRAME_SLOTS], block, sem.at[0])
                copy.start()
                copy.wait()
                first = jnp.where(side == 0, p, 1 - p) * HALF
                values = position_rows(block[PACK:])
                for part in range(2):
                    query = [feat[0], blank] if part == 0 else [blank, feat[0]]
                    scores = (
                        jnp.dot(block[:PACK], jnp.concatenate(query, axis=0), preferred_element_type=f32)
                        * SCORE_SCALE
                    )
                    index = lax.broadcasted_iota(jnp.int32, (PACK, HALF), 0) + first + part * PACK
                    there = index < count
                    before = stats[0:1]
                    peak = jnp.maximum(before, jnp.max(jnp.where(there, scores, -1e30), axis=0, keepdims=True))
                    mass = jnp.where(there, jnp.exp(scores - peak), 0.0)
                    top = mass.astype(bf16)
                    rest = (mass - top.astype(f32)).astype(bf16)
                    lhs = values[:, part * PACK : (part + 1) * PACK]
                    fresh = jnp.dot(lhs, top, preferred_element_type=f32) + jnp.dot(
                        lhs, rest, preferred_element_type=f32
                    )
                    stats[8:16] = stats[8:16] * jnp.exp(before - peak) + fresh
                    stats[0:8] = jnp.broadcast_to(peak, (8, HALF))
                return carry

            lax.fori_loop(0, 2, half_step, 0)
            mean = stats[8:11] / stats[11:12]
            share = sigma.astype(f32) / e.astype(f32)
            result[0:3] += jnp.where(live & usable, (mean - coords) * share, 0.0)
            return carry

        lax.fori_loop(0, FRAME_SLOTS, neighbour, 0)
        put_rows(lines, result[0:3] / terms.astype(f32), 0)
        copy = pltpu.make_async_copy(lines, out_ref, sem.at[0])
        copy.start()
        copy.wait()


def per_device(features, positions, counts):
    total = counts.shape[0]
    anywhere = pl.BlockSpec(memory_space=pl.ANY)
    fast, kept = pl.pallas_call(
        functools.partial(gather_and_match, total),
        out_shape=[
            jax.ShapeDtypeStruct((ROWS + FLAG_ROWS, 128), f32),
            jax.ShapeDtypeStruct((SLOTS, MSG, 128), bf16),
        ],
        in_specs=[anywhere, anywhere, anywhere],
        out_specs=[anywhere, anywhere],
        scratch_shapes=[
            pltpu.SMEM((total,), jnp.int32),
            pltpu.VMEM((1, CHANNELS, HALF), bf16),
            pltpu.VMEM((1, 3, HALF), bf16),
            pltpu.VMEM((MSG, 128), bf16),
            pltpu.VMEM((MSG, 128), bf16),
            pltpu.VMEM((SLOTS, MSG, 128), bf16),
            pltpu.VMEM((2 * CHANNELS, HALF), bf16),
            pltpu.VMEM((SLOTS, 8, HALF), f32),
            pltpu.SemaphoreType.DMA((SLOTS + 1,)),
            pltpu.SemaphoreType.DMA((SLOTS + 1,)),
            pltpu.SemaphoreType.DMA((SLOTS,)),
            pltpu.SemaphoreType.DMA((3,)),
            pltpu.SemaphoreType.REGULAR,
            pltpu.SemaphoreType.REGULAR,
            pltpu.VMEM((ROWS + FLAG_ROWS, 128), f32),
            pltpu.SemaphoreType.DMA,
        ],
        compiler_params=pltpu.CompilerParams(
            collective_id=0, has_side_effects=True, vmem_limit_bytes=56 * 2**20
        ),
        name="gather_and_match",
    )(counts, features, positions)
    flat = pl.pallas_call(
        functools.partial(finish, total),
        out_shape=jax.ShapeDtypeStruct((3 * HALF // 128, 128), f32),
        in_specs=[anywhere] * 5,
        out_specs=anywhere,
        scratch_shapes=[
            pltpu.SMEM((total,), jnp.int32),
            pltpu.VMEM((FLAG_ROWS, 128), f32),
            pltpu.VMEM((1, CHANNELS, HALF), bf16),
            pltpu.VMEM((1, 3, HALF), bf16),
            pltpu.VMEM((MSG, 128), bf16),
            pltpu.VMEM((16, HALF), f32),
            pltpu.VMEM((8, HALF), f32),
            pltpu.VMEM((ROWS, 128), f32),
            pltpu.SemaphoreType.DMA((2,)),
        ],
        compiler_params=pltpu.CompilerParams(vmem_limit_bytes=56 * 2**20),
        name="finish",
    )(counts, fast, features, positions, kept)
    return flat.reshape(1, 3, HALF)


def solution(mesh):
    in_specs = (P("tm", None, "pts"), P("tm", None, "pts"), P())
    out_specs = P("tm", None, "pts")
    return jax.shard_map(
        per_device, mesh=mesh, in_specs=in_specs, out_specs=out_specs, check_vma=False
    )
```

```python
import functools

import jax
import jax.numpy as jnp
from jax import lax
from jax.experimental import pallas as pl
from jax.experimental.pallas import tpu as pltpu
from jax.sharding import PartitionSpec as P

REACH = 3
CHANNELS = 64
HALF = 1024
PACK = HALF // 2
POS_ROWS = 32
MSG = PACK + POS_ROWS
ROWS = 3 * HALF // 128
FLAG_ROWS = HALF // 128
SCORE_SCALE = 0.25
LOG2E = 1.4426950408889634
DEN_LOW = 2.0**6
DEN_HIGH = 2.0**24
ROW_FRAMES = 16
MESH = pl.DeviceIdType.MESH
f32 = jnp.float32
bf16 = jnp.bfloat16
f8 = jnp.float8_e5m2

OFFSETS = (1, 2, -2, -1, 3, -3)
FRAME_SLOTS = len(OFFSETS)
SLOTS = 2 * FRAME_SLOTS
XM = SLOTS
ORDERS = (
    (0, 1, 2, 3, 4, 5, 6, 7, 8, 9, 10, 11),
    (0, 1, 4, 6, 2, 7, 3, 10, 8, 5, 9, 11),
    (0, 2, 3, 6, 5, 8, 1, 9, 4, 7, 10, 11),
    (0, 1, 2, 3, 4, 6, 7, 8, 9, 10, 5, 11),
    (0, 2, 3, 6, 5, 9, 8, 1, 4, 7, 11, 10),
    (0, 1, 4, 6, 7, 2, 10, 3, 8, 5, 9, 11),
    (0, 2, 3, 5, 8, 6, 9, 11, 1, 4, 7, 10),
)
KINDS = (1, 2, 3, 0, 0, 0, 0, 0, 0, 0, 0, 0, 0, 3, 4, 5)
RELAY_STEPS = {
    1: (1, 1, 5, 1, 7, 1, 8),
    2: (2, 4, 1, 2, 1, 5, 1),
    XM: (3, 3, 3, 3, 3, 3, 3),
    7: (7, 5, 9, 6, 9, 4, 10),
    8: (7, 8, 5, 7, 6, 8, 4),
}
BACK_STEP = 3
CROSS_STEP = 1


def inside(frame, total):
    return (frame >= 0) & (frame < total)


def pick(table, place):
    value = jnp.int32(table[-1])
    for index, entry in enumerate(table[:-1]):
        value = jnp.where(place == index, entry, value)
    return value


def other_row(a, b):
    return lax.div(a, ROW_FRAMES) != lax.div(b, ROW_FRAMES)


def pack_message(feat, pos, usable):
    kept = jnp.where(usable, feat.astype(f32), 0.0)
    rows = jnp.concatenate([kept[:, :PACK], kept[:, PACK:]], axis=0).astype(bf16).T
    flag = usable.astype(f32)
    quad = jnp.concatenate([jnp.where(usable, pos.astype(f32), 0.0), flag], axis=0)
    tail = jnp.concatenate([quad[:, q * 128 : (q + 1) * 128] for q in range(HALF // 128)], axis=0)
    return rows, tail.astype(bf16)


def position_rows(tail):
    tail = tail.astype(f32)
    pieces = []
    for j in range(POS_ROWS // 8):
        block = tail[j * 8 : j * 8 + 8]
        pieces.append(block)
        pieces.append(jnp.concatenate([block[4:], block[:4]], axis=0))
    return jnp.concatenate(pieces, axis=1).astype(bf16)


def put_rows(ref, values, first):
    for row in range(values.shape[0]):
        for q in range(HALF // 128):
            at = first + row * (HALF // 128) + q
            ref[at : at + 1] = values[row : row + 1, q * 128 : (q + 1) * 128]


def gather_and_match(
    total,
    cnt_in,
    feat_in,
    pos_in,
    out_ref,
    kept_ref,
    cnt_ref,
    feat_ref,
    pos_ref,
    own,
    xm,
    keys,
    weights,
    acc,
    send_sem,
    recv_sem,
    keep_sem,
    load_sem,
    half_ready,
    row_ready,
    result,
    result_sem,
):
    t = lax.axis_index("tm")
    p = lax.axis_index("pts")
    sigma = 1 - 2 * lax.rem(t, 2)
    sibling, across, near, far = t + sigma, t - sigma, t - 2 * sigma, t + 2 * sigma

    loads = [
        pltpu.make_async_copy(feat_in, feat_ref, load_sem.at[0]),
        pltpu.make_async_copy(pos_in, pos_ref, load_sem.at[1]),
        pltpu.make_async_copy(cnt_in, cnt_ref, load_sem.at[2]),
    ]
    for load in loads:
        load.start()

    barrier = pltpu.get_barrier_semaphore()
    pl.semaphore_signal(barrier, inc=1, device_id=(sibling, p), device_id_type=MESH)
    awaited = 1 + p
    above, below = jnp.int32(0), jnp.int32(0)

    @pl.when(p == 0)
    def _():
        pl.semaphore_signal(barrier, inc=1, device_id=(t, 1 - p), device_id_type=MESH)

    for frame in (across, near, far):
        there = inside(frame, total)
        crossing = there & other_row(t, frame)
        same = there & jnp.logical_not(other_row(t, frame))
        awaited = awaited + same.astype(jnp.int32)
        above = above + (crossing & (frame > t)).astype(jnp.int32)
        below = below + (crossing & (frame < t)).astype(jnp.int32)

        @pl.when(same | (crossing & (frame < t)))
        def _():
            pl.semaphore_signal(barrier, inc=1, device_id=(frame, p), device_id_type=MESH)

        @pl.when(crossing & (frame < t))
        def _():
            pl.semaphore_signal(barrier, inc=1, device_id=(frame, 1 - p), device_id_type=MESH)

    point = lax.broadcasted_iota(jnp.int32, (1, HALF), 1) + p * HALF
    for load in loads:
        load.wait()
    usable = point < cnt_ref[t]
    rows, tail = pack_message(feat_ref[0], pos_ref[0], usable)
    own[:PACK] = rows
    own[PACK:] = tail

    pl.semaphore_wait(barrier, awaited + 2 * above)

    @pl.when(p == 1)
    def _():
        pl.semaphore_signal(half_ready, inc=1, device_id=(t, 1 - p), device_id_type=MESH)

    for frame in (across, near, far):

        @pl.when(inside(frame, total) & other_row(t, frame) & (frame > t))
        def _():
            for half in (p, 1 - p):
                pl.semaphore_signal(row_ready, inc=1, device_id=(frame, half), device_id_type=MESH)


    def send(src, slot, frame, half, condition=True):
        dst = xm if slot == XM else keys.at[slot]

        @pl.when(inside(frame, total) & condition)
        def _():
            pltpu.make_async_remote_copy(
                src_ref=src,
                dst_ref=dst,
                send_sem=send_sem.at[slot],
                recv_sem=recv_sem.at[slot],
                device_id=(frame, half),
                device_id_type=MESH,
            ).start()

    def arrived(dst, slot):
        pltpu.make_async_copy(dst, dst, recv_sem.at[slot]).wait()

    near_crosses, far_crosses, across_crosses = (other_row(t, frame) for frame in (near, far, across))
    send(own, 0, sibling, p)
    send(own, 1, near, p, jnp.logical_not(near_crosses))
    send(own, 2, far, p, jnp.logical_not(far_crosses))
    send(own, XM, t, 1 - p, p == 1)

    scaled = feat_ref[0].astype(f32) * (SCORE_SCALE * LOG2E)
    high = scaled.astype(bf16)
    low = (scaled - high.astype(f32)).astype(bf16)
    weights[...] = jnp.concatenate([high, low], axis=0)

    def frame_of(slot):
        place = lax.rem(slot, FRAME_SLOTS)
        return t + sigma * pick(OFFSETS, place)

    place = lax.rem(t, ROW_FRAMES)
    kind = jnp.where(t == 1, 6, pick(KINDS, place))

    def relay(step, slot):
        due = step == pick(RELAY_STEPS[slot], kind)
        if slot == XM:

            @pl.when(due)
            def _():
                arrived(xm, XM)
                send(xm, 6, sibling, p)
                send(xm, 7, near, p, jnp.logical_not(near_crosses))
                send(xm, 8, far, p, jnp.logical_not(far_crosses))
                send(own, 7, near, 1 - p, near_crosses & (near > t))
                send(own, 8, far, 1 - p, far_crosses & (far > t))

            return

        @pl.when(due & inside(frame_of(slot), total))
        def _():
            arrived(keys.at[slot], slot)
            if slot in (1, 7):
                send(keys.at[slot], slot + 2, sibling, p)
                if slot == 1:
                    ready = jnp.logical_not(across_crosses) | (across > t)
                    send(keys.at[slot], 5, across, p, ready)
                    send(keys.at[slot], 11, across, 1 - p, across_crosses & ready)
                else:
                    send(keys.at[slot], 11, across, p, jnp.logical_not(across_crosses))
            else:
                send(keys.at[slot], slot + 2, sibling, p)

    def step(index, carry):
        @pl.when(index == CROSS_STEP)
        def _():
            send(own, 1, near, p, near_crosses & (near > t))
            send(own, 2, far, p, far_crosses & (far > t))

        @pl.when((index == 0) & (p == 0))
        def _():
            pl.semaphore_wait(half_ready, 1)
            send(own, XM, t, 1 - p)

        for slot in RELAY_STEPS:
            relay(index, slot)

        @pl.when((index == BACK_STEP) & (below > 0))
        def _():
            pl.semaphore_wait(row_ready, 2 * below)
            send(own, 1, near, p, near_crosses)
            send(own, 2, far, p, far_crosses)
            send(own, 7, near, 1 - p, near_crosses)
            send(own, 8, far, 1 - p, far_crosses)
            for slot, half in ((5, p), (11, 1 - p)):
                send(keys.at[1], slot, across, half, across_crosses)

        u = jnp.int32(0)
        for which, order in enumerate(ORDERS):
            u = jnp.where(kind == which, pick(order, index), u)

        @pl.when(inside(frame_of(u), total))
        def _():
            @pl.when((u != 1) & (u != 2) & (u != 7) & (u != 8))
            def _():
                arrived(keys.at[u], u)

            match(u)

        return carry

    def match(u):
        pltpu.make_async_copy(keys.at[u], kept_ref.at[u], keep_sem.at[u]).start()
        packed = keys[u, :PACK].astype(f32)
        turned = pltpu.roll(packed, CHANNELS, 1)
        left = lax.broadcasted_iota(jnp.int32, (PACK, 2 * CHANNELS), 1) < CHANNELS
        values = position_rows(keys[u, PACK:])
        highs, lows = [], []
        for half in range(2):
            points = jnp.where(left, packed, turned) if half == 0 else jnp.where(left, turned, packed)
            scores = jnp.dot(points.astype(bf16), weights[...], preferred_element_type=f32)
            mass = jnp.exp2(scores)
            top = mass.astype(bf16)
            highs.append(top)
            lows.append((mass - top.astype(f32)).astype(f8))
        acc[u] = jnp.dot(values, jnp.concatenate(highs, axis=0), preferred_element_type=f32) + jnp.dot(
            values.astype(f8), jnp.concatenate(lows, axis=0), preferred_element_type=f32
        )

    lax.fori_loop(0, SLOTS, step, 0)

    coords = pos_ref[0].astype(f32)
    velocity = jnp.zeros((3, HALF), f32)
    sound = jnp.ones((1, HALF), f32)
    terms = jnp.minimum(REACH, total - 1 - t) + jnp.minimum(REACH, t)
    for slot, e in enumerate(OFFSETS):
        summed = acc[slot] + acc[slot + FRAME_SLOTS]
        den = summed[3:4]
        live = inside(t + e * sigma, total)
        fine = jnp.where((den > DEN_LOW) & (den < DEN_HIGH), 1.0, 0.0)
        sound = jnp.where(live, jnp.minimum(sound, fine), sound)
        share = sigma.astype(f32) / e
        velocity = velocity + jnp.where(live, (summed[:3] / den - coords) * share, 0.0)
    put_rows(result, jnp.where(usable, velocity / terms.astype(f32), 0.0), 0)
    put_rows(result, jnp.where(usable, sound, 1.0), ROWS)
    leave = pltpu.make_async_copy(result, out_ref, result_sem)
    leave.start()

    def drain(slot, carry):
        @pl.when(inside(frame_of(slot), total))
        def _():
            pltpu.make_async_copy(keys.at[slot], kept_ref.at[slot], keep_sem.at[slot]).wait()

        return carry

    lax.fori_loop(0, SLOTS, drain, 0)

    def sent(slot, frame, condition=True):
        @pl.when(inside(frame, total) & condition)
        def _():
            pltpu.make_async_copy(own, own, send_sem.at[slot]).wait()

    ahead = inside(far, total)
    for side in (0, FRAME_SLOTS):
        sent(side + 0, sibling)
        sent(side + 1, near)
        sent(side + 2, far)
        sent(side + 3, sibling, ahead)
        sent(side + 4, sibling, inside(near, total))
        sent(side + 5, across, ahead)
    sent(XM, t)
    leave.wait()


def finish(
    total, cnt_in, fast_ref, feat_ref, pos_ref, kept_ref, out_ref, cnt_ref, flags, feat, pos, block, stats, result, lines, sem
):
    whole = pltpu.make_async_copy(fast_ref.at[pl.ds(0, ROWS)], out_ref, sem.at[0])
    check = pltpu.make_async_copy(fast_ref.at[pl.ds(ROWS, FLAG_ROWS)], flags, sem.at[1])
    check.start()
    whole.start()
    check.wait()
    sound = jnp.min(flags[...]) > 0.5
    whole.wait()

    @pl.when(jnp.logical_not(sound))
    def _():
        t = lax.axis_index("tm")
        p = lax.axis_index("pts")
        sigma = 1 - 2 * lax.rem(t, 2)
        for src, dst in ((feat_ref, feat), (pos_ref, pos), (cnt_in, cnt_ref)):
            copy = pltpu.make_async_copy(src, dst, sem.at[0])
            copy.start()
            copy.wait()
        coords = pos[0].astype(f32)
        blank = jnp.zeros((CHANNELS, HALF), bf16)
        usable = lax.broadcasted_iota(jnp.int32, (1, HALF), 1) + p * HALF < cnt_ref[t]
        result[...] = jnp.zeros((8, HALF), f32)
        terms = jnp.minimum(REACH, total - 1 - t) + jnp.minimum(REACH, t)

        def neighbour(slot, carry):
            e = pick(OFFSETS, slot)
            frame = t + e * sigma
            live = inside(frame, total)
            count = cnt_ref[jnp.clip(frame, 0, total - 1)]
            stats[0:8] = jnp.full((8, HALF), -1e30, f32)
            stats[8:16] = jnp.zeros((8, HALF), f32)

            def half_step(side, carry):
                copy = pltpu.make_async_copy(kept_ref.at[slot + side * FRAME_SLOTS], block, sem.at[0])
                copy.start()
                copy.wait()
                first = jnp.where(side == 0, p, 1 - p) * HALF
                values = position_rows(block[PACK:])
                for part in range(2):
                    query = [feat[0], blank] if part == 0 else [blank, feat[0]]
                    scores = (
                        jnp.dot(block[:PACK], jnp.concatenate(query, axis=0), preferred_element_type=f32)
                        * SCORE_SCALE
                    )
                    index = lax.broadcasted_iota(jnp.int32, (PACK, HALF), 0) + first + part * PACK
                    there = index < count
                    before = stats[0:1]
                    peak = jnp.maximum(before, jnp.max(jnp.where(there, scores, -1e30), axis=0, keepdims=True))
                    mass = jnp.where(there, jnp.exp(scores - peak), 0.0)
                    top = mass.astype(bf16)
                    rest = (mass - top.astype(f32)).astype(bf16)
                    lhs = values[:, part * PACK : (part + 1) * PACK]
                    fresh = jnp.dot(lhs, top, preferred_element_type=f32) + jnp.dot(
                        lhs, rest, preferred_element_type=f32
                    )
                    stats[8:16] = stats[8:16] * jnp.exp(before - peak) + fresh
                    stats[0:8] = jnp.broadcast_to(peak, (8, HALF))
                return carry

            lax.fori_loop(0, 2, half_step, 0)
            mean = stats[8:11] / stats[11:12]
            share = sigma.astype(f32) / e.astype(f32)
            result[0:3] += jnp.where(live & usable, (mean - coords) * share, 0.0)
            return carry

        lax.fori_loop(0, FRAME_SLOTS, neighbour, 0)
        put_rows(lines, result[0:3] / terms.astype(f32), 0)
        copy = pltpu.make_async_copy(lines, out_ref, sem.at[0])
        copy.start()
        copy.wait()


def per_device(features, positions, counts):
    total = counts.shape[0]
    anywhere = pl.BlockSpec(memory_space=pl.ANY)
    fast, kept = pl.pallas_call(
        functools.partial(gather_and_match, total),
        out_shape=[
            jax.ShapeDtypeStruct((ROWS + FLAG_ROWS, 128), f32),
            jax.ShapeDtypeStruct((SLOTS, MSG, 128), bf16),
        ],
        in_specs=[anywhere, anywhere, anywhere],
        out_specs=[anywhere, anywhere],
        scratch_shapes=[
            pltpu.SMEM((total,), jnp.int32),
            pltpu.VMEM((1, CHANNELS, HALF), bf16),
            pltpu.VMEM((1, 3, HALF), bf16),
            pltpu.VMEM((MSG, 128), bf16),
            pltpu.VMEM((MSG, 128), bf16),
            pltpu.VMEM((SLOTS, MSG, 128), bf16),
            pltpu.VMEM((2 * CHANNELS, HALF), bf16),
            pltpu.VMEM((SLOTS, 8, HALF), f32),
            pltpu.SemaphoreType.DMA((SLOTS + 1,)),
            pltpu.SemaphoreType.DMA((SLOTS + 1,)),
            pltpu.SemaphoreType.DMA((SLOTS,)),
            pltpu.SemaphoreType.DMA((3,)),
            pltpu.SemaphoreType.REGULAR,
            pltpu.SemaphoreType.REGULAR,
            pltpu.VMEM((ROWS + FLAG_ROWS, 128), f32),
            pltpu.SemaphoreType.DMA,
        ],
        compiler_params=pltpu.CompilerParams(
            collective_id=0, has_side_effects=True, vmem_limit_bytes=56 * 2**20
        ),
        name="gather_and_match",
    )(counts, features, positions)
    flat = pl.pallas_call(
        functools.partial(finish, total),
        out_shape=jax.ShapeDtypeStruct((3 * HALF // 128, 128), f32),
        in_specs=[anywhere] * 5,
        out_specs=anywhere,
        scratch_shapes=[
            pltpu.SMEM((total,), jnp.int32),
            pltpu.VMEM((FLAG_ROWS, 128), f32),
            pltpu.VMEM((1, CHANNELS, HALF), bf16),
            pltpu.VMEM((1, 3, HALF), bf16),
            pltpu.VMEM((MSG, 128), bf16),
            pltpu.VMEM((16, HALF), f32),
            pltpu.VMEM((8, HALF), f32),
            pltpu.VMEM((ROWS, 128), f32),
            pltpu.SemaphoreType.DMA((2,)),
        ],
        compiler_params=pltpu.CompilerParams(vmem_limit_bytes=56 * 2**20),
        name="finish",
    )(counts, fast, features, positions, kept)
    return flat.reshape(1, 3, HALF)


def solution(mesh):
    in_specs = (P("tm", None, "pts"), P("tm", None, "pts"), P())
    out_specs = P("tm", None, "pts")
    return jax.shard_map(
        per_device, mesh=mesh, in_specs=in_specs, out_specs=out_specs, check_vma=False
    )
```
